32 devices in a mesh: dp: 4 (over y, x), ctx: 8 (over z, core).
Axes of the slice: x: 2, y: 2, z: 4, core: 2. Of those that a mesh axis runs over, the one named last changes fastest.
Arguments:
- queries: bfloat16 [4096, 1024], P(('dp', 'ctx')), parts along dimension 0, may hold values from -8 to 8
- keys: bfloat16 [4096, 1024], P(('dp', 'ctx')), parts along dimension 0, may hold values from -6 to 6
- values: bfloat16 [4096, 1024], P(('dp', 'ctx')), parts along dimension 0, may hold values from -6 to 6
- cotangent: bfloat16 [4096, 1024], P(('dp', 'ctx')), parts along dimension 0, may hold values from -0.796875 to 0.796875
- out_weight: bfloat16 [1024, 1024], P('ctx'), may hold values from -0.75 to 0.75
Outputs:
- projected: bfloat16 [4096, 1024], P(('dp', 'ctx')), parts along dimension 0
- weight_grad: float32 [4096, 1024], P(('dp', 'ctx')), parts along dimension 0
- query_grad: bfloat16 [4096, 1024], P(('dp', 'ctx')), parts along dimension 0
- key_grad: bfloat16 [4096, 1024], P(('dp', 'ctx')), parts along dimension 0
- value_grad: bfloat16 [4096, 1024], P(('dp', 'ctx')), parts along dimension 0
The draws below stay inside these ranges and needn't reach their ends.
There are 4 independent parts, one for each index of `dp`. The reference program is written for one: setup_inputs(seed, part) draws one part's arguments, and reference() takes and returns one part's arrays. A program takes and returns all parts, laid end to end along the dimension named above; an argument that names none is the same for every part. Nothing has to cross between parts.
All inputs are finite; a program needn't handle non-finite values.
Results may differ from the reference program's by a relative error of at most 0.034.
Values may be sent and summed in bfloat16 or wider, within the bound.
A program may use at most 64 MiB of HBM per device.

```python
import jax
import jax.numpy as jnp
from jax import lax

D = 1024
H = 16
DH = 64
R = 16
SEG = 512
KEYS = 32
TOKENS = 1024


def draw_queries(key, part):
    key = jax.random.fold_in(key, 3)
    sampled = jnp.clip(2.5 * jax.random.normal(key, (TOKENS, D), jnp.float32), -8.0, 8.0)
    return sampled.astype(jnp.bfloat16)


def draw_keys(key, part):
    key = jax.random.fold_in(key, 5)
    sampled = jnp.clip(jax.random.normal(key, (TOKENS, D), jnp.float32), -6.0, 6.0)
    return sampled.astype(jnp.bfloat16)


def strengthened(entries, stream_key, source, target, parts, factor):
    owner, partner = [(jnp.arange(entries.shape[axis_at]) // (entries.shape[axis_at] // parts)).reshape([-1 if axis == axis_at else 1 for axis in range(entries.ndim)]) for axis_at in (source, target)]
    chosen = jax.random.permutation(stream_key, parts)[partner]
    strong = (owner == chosen) | (owner == (partner + parts // 2) % parts)
    return jnp.where(strong, factor * entries, entries)


def level_of(own_key, shape, split, smallest, largest):
    level = 1.0
    for dim, blocks in split:
        heights = jax.random.uniform(jax.random.fold_in(jax.random.fold_in(own_key, 6), dim), (blocks,), jnp.float32, smallest / len(split), largest / len(split))
        level = level * jnp.repeat(jnp.exp(heights), shape[dim] // blocks).reshape((-1,) + (1,) * (len(shape) - 1 - dim))
    return level


def centred(own_key, extent, deviation, reach, cuts=(), kind=jnp.bfloat16):
    gain = level_of(own_key, extent, cuts, -0.22, 0.18) if cuts else 1.0
    drawn = jax.random.normal(own_key, extent, jnp.float32) * deviation * gain
    return jnp.minimum(jnp.maximum(drawn, -reach), reach).astype(kind)


def heavy_noise(own_key, dims, scale, bound, split, heavy, kind=jnp.bfloat16):
    entries = scale * jax.random.normal(own_key, dims, jnp.float32)
    if split:
        entries = entries * level_of(own_key, dims, split, -0.22, 0.18)
    return jnp.clip(strengthened(entries, jax.random.fold_in(own_key, 3), *heavy), -bound, bound).astype(kind)


def setup_inputs(seed: int = 0, part: int = 0) -> dict:
    seeds = jax.random.split(jax.random.key(seed), 6)
    part_keys = jax.random.split(jax.random.fold_in(seeds[5], part), 6)
    queries = draw_queries(jax.random.fold_in(jax.random.fold_in(seeds[5], part), 71), part)
    keys = draw_keys(jax.random.fold_in(jax.random.fold_in(seeds[5], part), 71), part)
    values = centred(part_keys[2], (TOKENS, D), 1.0, 6.0, ((0, 8),))
    cotangent = heavy_noise(part_keys[3], (TOKENS, D), 0.1, 0.796875, ((0, 8),), (0, 1, 8, 2.0))
    out_weight = centred(seeds[4], (D, D), DH ** -0.5, 0.75, ((0, 8),))
    return {"queries": queries, "keys": keys, "values": values, "cotangent": cotangent, "out_weight": out_weight}


def select_mask(dtype):
    residue = jnp.arange(R)[:, None]
    head_ids = jnp.arange(H)[None, :]
    return (head_ids % R == residue).astype(dtype)[:, :, None]


def sparse_rows(full_rows):
    reshaped = full_rows.reshape(full_rows.shape[0] // R, R, H, DH)
    return jnp.sum(reshaped * select_mask(full_rows.dtype), axis=1)


def dense_rows(sparse):
    placed = sparse[:, None, :, :] * select_mask(sparse.dtype)
    return placed.reshape(sparse.shape[0] * R, H * DH)


def rounded(array):
    return lax.optimization_barrier(array.astype(jnp.bfloat16)).astype(jnp.float32)


def reference(queries, keys, values, cotangent, out_weight):
    score_scale = DH ** -0.5
    seg_count = TOKENS // SEG
    q_blocks = sparse_rows(queries).reshape(seg_count, KEYS, H, DH)
    k_blocks = sparse_rows(keys).reshape(seg_count, KEYS, H, DH)
    v_blocks = sparse_rows(values).reshape(seg_count, KEYS, H, DH)

    def forward(pieces):
        q_blk, k_blk, v_blk = pieces
        scores = jnp.einsum("qhd,khd->hqk", q_blk.astype(jnp.float32), k_blk.astype(jnp.float32)) * score_scale
        row_top = jnp.max(scores, axis=-1, keepdims=True)
        log_total = row_top + jnp.log(jnp.sum(jnp.exp(scores - row_top), axis=-1, keepdims=True))
        probability = rounded(jnp.exp(scores - log_total))
        attn_blk = jnp.einsum("hqk,khd->qhd", probability, v_blk.astype(jnp.float32)).astype(jnp.bfloat16)
        return attn_blk, log_total

    attn_blocks, totals = lax.map(forward, (q_blocks, k_blocks, v_blocks))
    attention = dense_rows(attn_blocks.reshape(seg_count * KEYS, H, DH))
    projected = jnp.dot(attention, out_weight.T, preferred_element_type=jnp.float32).astype(jnp.bfloat16)
    weight_grad = jnp.dot(cotangent.T, attention, preferred_element_type=jnp.float32)
    d_attention = jnp.dot(cotangent, out_weight, preferred_element_type=jnp.float32).astype(jnp.bfloat16)
    da_blocks = sparse_rows(d_attention).reshape(seg_count, KEYS, H, DH)

    def backward(pieces):
        q_blk, k_blk, v_blk, da_blk, attn_blk, log_total = pieces
        q_wide = q_blk.astype(jnp.float32)
        k_wide = k_blk.astype(jnp.float32)
        v_wide = v_blk.astype(jnp.float32)
        da_wide = da_blk.astype(jnp.float32)
        scores = jnp.einsum("qhd,khd->hqk", q_wide, k_wide) * score_scale
        probability = jnp.exp(scores - log_total)
        row_delta = jnp.sum(da_wide * attn_blk.astype(jnp.float32), axis=-1)
        prob_grad = jnp.einsum("qhd,khd->hqk", da_wide, v_wide)
        score_grad = rounded(probability * (prob_grad - row_delta.T[:, :, None]))
        query_part = (jnp.einsum("hqk,khd->qhd", score_grad, k_wide) * score_scale).astype(jnp.bfloat16)
        key_part = (jnp.einsum("hqk,qhd->khd", score_grad, q_wide) * score_scale).astype(jnp.bfloat16)
        value_part = jnp.einsum("hqk,qhd->khd", rounded(probability), da_wide).astype(jnp.bfloat16)
        return query_part, key_part, value_part

    query_parts, key_parts, value_parts = lax.map(backward, (q_blocks, k_blocks, v_blocks, da_blocks, attn_blocks, totals))
    shape_flat = (seg_count * KEYS, H, DH)
    query_grad = dense_rows(query_parts.reshape(shape_flat))
    key_grad = dense_rows(key_parts.reshape(shape_flat))
    value_grad = dense_rows(value_parts.reshape(shape_flat))
    return (projected, weight_grad, query_grad, key_grad, value_grad)
```

```python
import functools

import jax
import jax.numpy as jnp
from jax import lax
from jax.experimental import pallas as pl
from jax.experimental.pallas import tpu as pltpu
from jax.sharding import PartitionSpec as P

H = 16
DH = 64
R = 16


def partner_2(value, axis, apart):
    mask = 2**apart
    pairs = [(source, source ^ mask) for source in range(lax.axis_size(axis))]
    return lax.ppermute(value, axis, pairs)


def select_mask(dtype):
    residue = jnp.arange(R)[:, None]
    head_ids = jnp.arange(H)[None, :]
    return (head_ids % R == residue).astype(dtype)[:, :, None]


def sparse_rows(full_rows):
    reshaped = full_rows.reshape(full_rows.shape[0] // R, R, H, DH)
    return jnp.sum(reshaped * select_mask(full_rows.dtype), axis=1)


def dense_rows(sparse):
    placed = sparse[:, None, :, :] * select_mask(sparse.dtype)
    return placed.reshape(sparse.shape[0] * R, H * DH)


def spread(payload, swapper, bit_list, device_index):
    visited = []
    gathered = payload
    for bit_num in bit_list:
        partner = swapper(gathered, bit_num)
        upper_half = device_index // (1 << bit_num) % 2 == 1
        gathered = jnp.where(
            upper_half, jnp.stack([partner, gathered]), jnp.stack([gathered, partner])
        )
        visited.insert(0, bit_num)
    axis_order = [visited.index(bit_num) for bit_num in sorted(visited, reverse=True)]
    trailing = list(range(len(visited), gathered.ndim))
    gathered = jnp.transpose(gathered, axis_order + trailing)
    return gathered.reshape((-1,) + payload.shape[1:])


def shards(queries, keys, values, cotangent, out_weight):
    ctx_size = lax.axis_size("ctx")
    seg_devices = min(64, ctx_size // 2)
    seg_bits = seg_devices.bit_length() - 1
    device_index = lax.axis_index("ctx")
    bit_list = list(range(seg_bits))
    score_scale = DH ** (-0.5)
    q_sparse = sparse_rows(queries)
    k_sparse = sparse_rows(keys)
    v_sparse = sparse_rows(values)
    gathered = spread(
        jnp.stack([k_sparse, v_sparse], axis=1),
        lambda payload, bit_num: partner_2(payload, "ctx", bit_num),
        bit_list,
        device_index,
    )
    seg_keys = gathered[:, 0]
    seg_values = gathered[:, 1]
    full_weight = lax.all_gather(out_weight, "ctx", axis=0, tiled=True)
    scores = (
        jnp.einsum("qhd,khd->hqk", q_sparse, seg_keys, preferred_element_type=jnp.float32)
        * score_scale
    )
    row_top = jnp.max(scores, axis=-1, keepdims=True)
    log_total = row_top + jnp.log(jnp.sum(jnp.exp(scores - row_top), axis=-1, keepdims=True))
    probability = jnp.exp(scores - log_total)
    attn_sparse = jnp.einsum(
        "hqk,khd->qhd",
        probability.astype(jnp.bfloat16),
        seg_values,
        preferred_element_type=jnp.float32,
    ).astype(jnp.bfloat16)
    attention = dense_rows(attn_sparse)
    projected = lax.dot_general(
        attention, full_weight, (((1,), (1,)), ((), ())), preferred_element_type=jnp.float32
    ).astype(jnp.bfloat16)
    weight_grad = lax.psum_scatter(
        lax.dot_general(
            cotangent, attention, (((0,), (0,)), ((), ())), preferred_element_type=jnp.float32
        ),
        "ctx",
        scatter_dimension=0,
        tiled=True,
    )
    d_attention = jnp.dot(cotangent, full_weight, preferred_element_type=jnp.float32).astype(
        jnp.bfloat16
    )
    da_sparse = sparse_rows(d_attention)
    row_delta = jnp.sum(da_sparse.astype(jnp.float32) * attn_sparse.astype(jnp.float32), axis=-1)
    prob_grad = jnp.einsum(
        "qhd,khd->hqk", da_sparse, seg_values, preferred_element_type=jnp.float32
    )
    score_grad = (probability * (prob_grad - row_delta.T[:, :, None])).astype(jnp.bfloat16)
    query_part = (
        jnp.einsum("hqk,khd->qhd", score_grad, seg_keys, preferred_element_type=jnp.float32)
        * score_scale
    ).astype(jnp.bfloat16)
    row_stats = jnp.stack([log_total[:, :, 0].T, row_delta], axis=1)
    seg_stats = spread(
        row_stats,
        lambda payload, bit_num: partner_2(payload, "ctx", bit_num),
        bit_list,
        device_index,
    )
    paired = spread(
        jnp.stack([q_sparse, da_sparse], axis=1),
        lambda payload, bit_num: partner_2(payload, "ctx", bit_num),
        bit_list,
        device_index,
    )
    seg_queries = paired[:, 0]
    seg_cotangent = paired[:, 1]
    key_scores = (
        jnp.einsum("qhd,khd->hqk", seg_queries, k_sparse, preferred_element_type=jnp.float32)
        * score_scale
    )
    key_prob = jnp.exp(key_scores - seg_stats[:, 0].T[:, :, None])
    key_dgrad = jnp.einsum(
        "qhd,khd->hqk", seg_cotangent, v_sparse, preferred_element_type=jnp.float32
    )
    key_dscore = (key_prob * (key_dgrad - seg_stats[:, 1].T[:, :, None])).astype(jnp.bfloat16)
    key_part = (
        jnp.einsum("hqk,qhd->khd", key_dscore, seg_queries, preferred_element_type=jnp.float32)
        * score_scale
    ).astype(jnp.bfloat16)
    value_part = jnp.einsum(
        "hqk,qhd->khd",
        key_prob.astype(jnp.bfloat16),
        seg_cotangent,
        preferred_element_type=jnp.float32,
    ).astype(jnp.bfloat16)
    return (
        projected,
        weight_grad,
        dense_rows(query_part),
        dense_rows(key_part),
        dense_rows(value_part),
    )


LANES = 128
D = H * DH
F32 = jnp.float32
BF16 = jnp.bfloat16


def fits(mesh):
    return mesh.shape["ctx"] * LANES == D


def mm(a, b, dims):
    return lax.dot_general(a, b, (dims, ((), ())), preferred_element_type=F32)


NN = ((1,), (0,))
NT = ((1,), (1,))
TN = ((0,), (0,))


def fused_kernel(
    n, rows,
    q_hbm, k_hbm, v_hbm, c_hbm, w_hbm,
    proj_hbm, wg_hbm, dq_hbm, dk_hbm, dv_hbm,
    q_v, k_v, v_v, c_v, w_v,
    qkv_send, qkv_recv, cot_send, cot_recv, attn_recv, da_send, da_recv,
    pr_send, pr_recv, dg_send, dg_recv, attn2,
    pr_out, wg_out, dq_out, dk_out, dv_out,
    send_sem, recv_sem, in_sem, out_sem,
):
    per = rows // R
    group = 2 * per
    seg_devices = n // 2
    total = n * per
    me = lax.axis_index("ctx")
    peers = [lax.rem(me + d, n) for d in range(n)]
    sources = [lax.rem(me + n - d, n) for d in range(n)]

    barrier = pltpu.get_barrier_semaphore()
    for d in range(1, n):
        pl.semaphore_signal(
            barrier, inc=1, device_id={"ctx": peers[d]}, device_id_type=pl.DeviceIdType.MESH
        )
    loads = [
        pltpu.make_async_copy(src, dst, in_sem.at[i])
        for i, (src, dst) in enumerate(
            [(q_hbm, q_v), (k_hbm, k_v), (v_hbm, v_v), (c_hbm, c_v), (w_hbm, w_v)]
        )
    ]
    for load in loads:
        load.start()

    def remote(kind, d, src, dst):
        return pltpu.make_async_remote_copy(
            src_ref=src,
            dst_ref=dst,
            send_sem=send_sem.at[kind, d],
            recv_sem=recv_sem.at[kind, d],
            device_id={"ctx": peers[d]},
            device_id_type=pl.DeviceIdType.MESH,
        )

    row_id = lax.broadcasted_iota(jnp.int32, (rows, rows), 0)
    col_id = lax.broadcasted_iota(jnp.int32, (rows, rows), 1)
    order = (col_id == R * (row_id % per) + row_id // per).astype(F32).astype(BF16)
    left_row = lax.broadcasted_iota(jnp.int32, (1, LANES), 1) < DH

    for load in loads[:3]:
        load.wait()
    for c in range(n):
        cols = pl.ds(c * LANES, LANES)
        picker = order[c * group : (c + 1) * group, :]
        parts = []
        for ref in (q_v, k_v, v_v):
            picked = mm(picker, ref[:, cols], NN)
            parts.append(jnp.where(left_row, picked[:per], picked[per:]))
        parts.append(jnp.zeros_like(parts[0]))
        qkv_send[c] = jnp.concatenate(parts, axis=0).astype(BF16)
    loads[3].wait()
    for c in range(n):
        cols = pl.ds(c * LANES, LANES)
        cot_send[c] = mm(order, c_v[:, cols], NN).astype(BF16)
    qkv_recv[me] = qkv_send[me]
    cot_recv[me] = cot_send[me]

    pl.semaphore_wait(barrier, n - 1)
    qkv_copies = [remote(0, d, qkv_send.at[peers[d]], qkv_recv.at[me]) for d in range(1, n)]
    cot_copies = [remote(1, d, cot_send.at[peers[d]], cot_recv.at[me]) for d in range(1, n)]
    for copy in qkv_copies:
        copy.start()
    for copy in cot_copies:
        copy.start()
    loads[4].wait()

    for copy in qkv_copies:
        copy.wait_recv()
    got = qkv_recv[...].astype(F32)

    def taken(j):
        return got[:, j * per : (j + 1) * per, :].reshape(total, LANES)

    def split(x):
        zero = jnp.zeros_like(x)
        return jnp.concatenate(
            [jnp.where(left_row, x, zero), jnp.where(left_row, zero, x)], axis=0
        )

    def joined(x):
        return jnp.where(left_row, x[:total], x[total:])

    scale = DH ** (-0.5)
    q_two = split(taken(0)).astype(BF16)
    k_all = taken(1).astype(BF16)
    v_all = taken(2).astype(BF16)
    seg_rows = seg_devices * per
    q_seg = (lax.broadcasted_iota(jnp.int32, (2 * total, total), 0) % total) // seg_rows
    k_seg = lax.broadcasted_iota(jnp.int32, (2 * total, total), 1) // seg_rows
    same = q_seg == k_seg
    scores = jnp.where(same, mm(q_two, k_all, NT) * scale, -jnp.inf)
    raised = jnp.exp(scores - jnp.max(scores, axis=-1, keepdims=True))
    prob = raised / jnp.sum(raised, axis=-1, keepdims=True)
    prob_16 = prob.astype(BF16)
    attn = joined(mm(prob_16, v_all, NN)).astype(BF16)
    attn_recv[me] = attn
    attn_copies = [remote(2, d, attn_recv.at[me], attn_recv.at[me]) for d in range(1, n)]
    for copy in attn_copies:
        copy.start()

    for copy in cot_copies:
        copy.wait_recv()

    def cot_group(c):
        picked = cot_recv[:, pl.ds(pl.multiple_of(c * group, group), group), :]
        return picked.reshape(n * group, LANES)

    def tile(c):
        return pl.ds(pl.multiple_of(c * LANES, LANES), LANES)

    da_copies = []
    own_da = None
    for d in list(range(1, n)) + [0]:
        c = peers[d]
        both = mm(cot_group(c), w_v[:, tile(c)], NN).reshape(n, 2, per, LANES)
        share = jnp.where(left_row, both[:, 0], both[:, 1]).reshape(total, LANES)
        if d == 0:
            own_da = share
            continue
        da_send[d] = share.astype(BF16)
        copy = remote(3, d, da_send.at[d], da_recv.at[d])
        copy.start()
        da_copies.append(copy)

    for d in range(n):
        c = sources[d]
        if d:
            attn_copies[d - 1].wait_recv()
        packed = attn_recv[c].astype(F32).reshape(n, per, LANES)
        zero = jnp.zeros_like(packed)
        wide = jnp.stack([jnp.where(left_row, packed, zero), jnp.where(left_row, zero, packed)], axis=1)
        wide = wide.reshape(n * group, LANES).astype(BF16)
        attn2[d] = wide
        out = mm(wide, w_v[:, tile(c)], NT).astype(BF16)
        pr_send[:, pl.ds(pl.multiple_of(c * group, group), group), :] = out.reshape(n, group, LANES)
    pr_recv[me] = pr_send[me]
    pr_copies = [remote(4, d, pr_send.at[peers[d]], pr_recv.at[me]) for d in range(1, n)]
    for copy in pr_copies:
        copy.start()

    for copy in da_copies:
        copy.wait_recv()
    da = own_da
    for d in range(1, n):
        da = da + da_recv[d].astype(F32)
    da_two = split(da).astype(BF16)
    attn_two = split(attn.astype(F32))
    delta = jnp.sum(da_two.astype(F32) * attn_two, axis=-1, keepdims=True)
    d_score = (prob * (mm(da_two, v_all, NT) - delta)).astype(BF16)
    dq = joined(mm(d_score, k_all, NN)) * scale
    dk = mm(d_score, q_two, TN) * scale
    dv = mm(prob_16, da_two, TN)
    grads = [g.reshape(n, per, LANES) for g in (dq, dk, dv)]
    grads.append(jnp.zeros_like(grads[0]))
    dg_send[...] = jnp.concatenate(grads, axis=1).astype(BF16)
    dg_recv[me] = dg_send[me]
    dg_copies = [remote(5, d, dg_send.at[peers[d]], dg_recv.at[me]) for d in range(1, n)]
    for copy in dg_copies:
        copy.start()

    for d in range(n):
        c = sources[d]
        wg_out[:, tile(c)] = mm(cot_group(c), attn2[d], TN)
    stores = [
        pltpu.make_async_copy(src, dst, out_sem.at[i])
        for i, (src, dst) in enumerate(
            [(wg_out, wg_hbm), (pr_out, proj_hbm), (dq_out, dq_hbm), (dk_out, dk_hbm), (dv_out, dv_hbm)]
        )
    ]
    stores[0].start()

    for copy in pr_copies:
        copy.wait_recv()
    for c in range(n):
        pr_out[:, c * LANES : (c + 1) * LANES] = mm(order, pr_recv[c], TN).astype(BF16)
    stores[1].start()

    for copy in dg_copies:
        copy.wait_recv()
    head = lax.broadcasted_iota(jnp.int32, (R, LANES), 0)
    lane_head = lax.broadcasted_iota(jnp.int32, (R, LANES), 1) // DH
    for j, out in enumerate((dq_out, dk_out, dv_out)):
        for c in range(n):
            block = dg_recv[c].astype(F32)[j * per : (j + 1) * per]
            here = (lane_head + 2 * c == head)[None]
            spread_out = jnp.where(here, block[:, None, :], 0.0)
            out[:, c * LANES : (c + 1) * LANES] = spread_out.reshape(rows, LANES).astype(BF16)
        stores[2 + j].start()
    for copy in qkv_copies + cot_copies + attn_copies + da_copies + pr_copies + dg_copies:
        copy.wait_send()
    for store in stores:
        store.wait()


def fused(queries, keys, values, cotangent, out_weight):
    n = lax.axis_size("ctx")
    rows = queries.shape[0]
    per = rows // R
    total = n * per
    full = (rows, D)
    square = (n, rows, LANES)
    anywhere = pl.BlockSpec(memory_space=pl.ANY)
    return pl.pallas_call(
        functools.partial(fused_kernel, n, rows),
        out_shape=(
            jax.ShapeDtypeStruct(full, BF16),
            jax.ShapeDtypeStruct((D // n, D), F32),
            jax.ShapeDtypeStruct(full, BF16),
            jax.ShapeDtypeStruct(full, BF16),
            jax.ShapeDtypeStruct(full, BF16),
        ),
        in_specs=[anywhere] * 5,
        out_specs=[anywhere] * 5,
        scratch_shapes=[pltpu.VMEM(full, BF16)] * 4
        + [pltpu.VMEM((D // n, D), BF16)]
        + [
            pltpu.VMEM((n, 4 * per, LANES), BF16),
            pltpu.VMEM((n, 4 * per, LANES), BF16),
            pltpu.VMEM(square, BF16),
            pltpu.VMEM(square, BF16),
            pltpu.VMEM((n, total, LANES), BF16),
            pltpu.VMEM((n, total, LANES), BF16),
            pltpu.VMEM((n, total, LANES), BF16),
            pltpu.VMEM(square, BF16),
            pltpu.VMEM(square, BF16),
            pltpu.VMEM((n, 4 * per, LANES), BF16),
            pltpu.VMEM((n, 4 * per, LANES), BF16),
            pltpu.VMEM((n, n * 2 * per, LANES), BF16),
            pltpu.VMEM(full, BF16),
            pltpu.VMEM((D // n, D), F32),
            pltpu.VMEM(full, BF16),
            pltpu.VMEM(full, BF16),
            pltpu.VMEM(full, BF16),
            pltpu.SemaphoreType.DMA((6, n)),
            pltpu.SemaphoreType.DMA((6, n)),
            pltpu.SemaphoreType.DMA((5,)),
            pltpu.SemaphoreType.DMA((5,)),
        ],
        compiler_params=pltpu.CompilerParams(
            collective_id=0, has_side_effects=True, vmem_limit_bytes=40 * 1024 * 1024
        ),
    )(queries, keys, values, cotangent, out_weight)


def solution(mesh):
    in_specs = (
        P(("dp", "ctx"), None),
        P(("dp", "ctx"), None),
        P(("dp", "ctx"), None),
        P(("dp", "ctx"), None),
        P("ctx", None),
    )
    out_specs = (
        P(("dp", "ctx"), None),
        P(("dp", "ctx"), None),
        P(("dp", "ctx"), None),
        P(("dp", "ctx"), None),
        P(("dp", "ctx"), None),
    )
    body = fused if fits(mesh) else shards
    return jax.shard_map(body, mesh=mesh, in_specs=in_specs, out_specs=out_specs, check_vma=False)
```

```python
import functools

import jax
import jax.numpy as jnp
from jax import lax
from jax.experimental import pallas as pl
from jax.experimental.pallas import tpu as pltpu
from jax.sharding import PartitionSpec as P

H = 16
DH = 64
R = 16


def partner_2(value, axis, apart):
    mask = 2**apart
    pairs = [(source, source ^ mask) for source in range(lax.axis_size(axis))]
    return lax.ppermute(value, axis, pairs)


def select_mask(dtype):
    residue = jnp.arange(R)[:, None]
    head_ids = jnp.arange(H)[None, :]
    return (head_ids % R == residue).astype(dtype)[:, :, None]


def sparse_rows(full_rows):
    reshaped = full_rows.reshape(full_rows.shape[0] // R, R, H, DH)
    return jnp.sum(reshaped * select_mask(full_rows.dtype), axis=1)


def dense_rows(sparse):
    placed = sparse[:, None, :, :] * select_mask(sparse.dtype)
    return placed.reshape(sparse.shape[0] * R, H * DH)


def spread(payload, swapper, bit_list, device_index):
    visited = []
    gathered = payload
    for bit_num in bit_list:
        partner = swapper(gathered, bit_num)
        upper_half = device_index // (1 << bit_num) % 2 == 1
        gathered = jnp.where(
            upper_half, jnp.stack([partner, gathered]), jnp.stack([gathered, partner])
        )
        visited.insert(0, bit_num)
    axis_order = [visited.index(bit_num) for bit_num in sorted(visited, reverse=True)]
    trailing = list(range(len(visited), gathered.ndim))
    gathered = jnp.transpose(gathered, axis_order + trailing)
    return gathered.reshape((-1,) + payload.shape[1:])


def shards(queries, keys, values, cotangent, out_weight):
    ctx_size = lax.axis_size("ctx")
    seg_devices = min(64, ctx_size // 2)
    seg_bits = seg_devices.bit_length() - 1
    device_index = lax.axis_index("ctx")
    bit_list = list(range(seg_bits))
    score_scale = DH ** (-0.5)
    q_sparse = sparse_rows(queries)
    k_sparse = sparse_rows(keys)
    v_sparse = sparse_rows(values)
    gathered = spread(
        jnp.stack([k_sparse, v_sparse], axis=1),
        lambda payload, bit_num: partner_2(payload, "ctx", bit_num),
        bit_list,
        device_index,
    )
    seg_keys = gathered[:, 0]
    seg_values = gathered[:, 1]
    full_weight = lax.all_gather(out_weight, "ctx", axis=0, tiled=True)
    scores = (
        jnp.einsum("qhd,khd->hqk", q_sparse, seg_keys, preferred_element_type=jnp.float32)
        * score_scale
    )
    row_top = jnp.max(scores, axis=-1, keepdims=True)
    log_total = row_top + jnp.log(jnp.sum(jnp.exp(scores - row_top), axis=-1, keepdims=True))
    probability = jnp.exp(scores - log_total)
    attn_sparse = jnp.einsum(
        "hqk,khd->qhd",
        probability.astype(jnp.bfloat16),
        seg_values,
        preferred_element_type=jnp.float32,
    ).astype(jnp.bfloat16)
    attention = dense_rows(attn_sparse)
    projected = lax.dot_general(
        attention, full_weight, (((1,), (1,)), ((), ())), preferred_element_type=jnp.float32
    ).astype(jnp.bfloat16)
    weight_grad = lax.psum_scatter(
        lax.dot_general(
            cotangent, attention, (((0,), (0,)), ((), ())), preferred_element_type=jnp.float32
        ),
        "ctx",
        scatter_dimension=0,
        tiled=True,
    )
    d_attention = jnp.dot(cotangent, full_weight, preferred_element_type=jnp.float32).astype(
        jnp.bfloat16
    )
    da_sparse = sparse_rows(d_attention)
    row_delta = jnp.sum(da_sparse.astype(jnp.float32) * attn_sparse.astype(jnp.float32), axis=-1)
    prob_grad = jnp.einsum(
        "qhd,khd->hqk", da_sparse, seg_values, preferred_element_type=jnp.float32
    )
    score_grad = (probability * (prob_grad - row_delta.T[:, :, None])).astype(jnp.bfloat16)
    query_part = (
        jnp.einsum("hqk,khd->qhd", score_grad, seg_keys, preferred_element_type=jnp.float32)
        * score_scale
    ).astype(jnp.bfloat16)
    row_stats = jnp.stack([log_total[:, :, 0].T, row_delta], axis=1)
    seg_stats = spread(
        row_stats,
        lambda payload, bit_num: partner_2(payload, "ctx", bit_num),
        bit_list,
        device_index,
    )
    paired = spread(
        jnp.stack([q_sparse, da_sparse], axis=1),
        lambda payload, bit_num: partner_2(payload, "ctx", bit_num),
        bit_list,
        device_index,
    )
    seg_queries = paired[:, 0]
    seg_cotangent = paired[:, 1]
    key_scores = (
        jnp.einsum("qhd,khd->hqk", seg_queries, k_sparse, preferred_element_type=jnp.float32)
        * score_scale
    )
    key_prob = jnp.exp(key_scores - seg_stats[:, 0].T[:, :, None])
    key_dgrad = jnp.einsum(
        "qhd,khd->hqk", seg_cotangent, v_sparse, preferred_element_type=jnp.float32
    )
    key_dscore = (key_prob * (key_dgrad - seg_stats[:, 1].T[:, :, None])).astype(jnp.bfloat16)
    key_part = (
        jnp.einsum("hqk,qhd->khd", key_dscore, seg_queries, preferred_element_type=jnp.float32)
        * score_scale
    ).astype(jnp.bfloat16)
    value_part = jnp.einsum(
        "hqk,qhd->khd",
        key_prob.astype(jnp.bfloat16),
        seg_cotangent,
        preferred_element_type=jnp.float32,
    ).astype(jnp.bfloat16)
    return (
        projected,
        weight_grad,
        dense_rows(query_part),
        dense_rows(key_part),
        dense_rows(value_part),
    )


LANES = 128
D = H * DH
F32 = jnp.float32
BF16 = jnp.bfloat16


def fits(mesh):
    return mesh.shape["ctx"] * LANES == D


def mm(a, b, dims):
    return lax.dot_general(a, b, (dims, ((), ())), preferred_element_type=F32)


NN = ((1,), (0,))
NT = ((1,), (1,))
TN = ((0,), (0,))


def fused_kernel(
    n, rows,
    q_hbm, k_hbm, v_hbm, c_hbm, w_hbm,
    pr_recv, dg_recv, wg_any,
    q_v, k_v, v_v, c_v, w_v,
    qkv_send, qkv_recv, cot_send, cot_recv, attn_recv, da_send, da_recv,
    pr_send, dg_send, attn2, wg_out,
    send_sem, recv_sem, in_sem, out_sem,
):
    per = rows // R
    group = 2 * per
    seg_devices = n // 2
    total = n * per
    me = lax.axis_index("ctx")
    peers = [lax.rem(me + d, n) for d in range(n)]
    sources = [lax.rem(me + n - d, n) for d in range(n)]

    barrier = pltpu.get_barrier_semaphore()
    for d in range(1, n):
        pl.semaphore_signal(
            barrier, inc=1, device_id={"ctx": peers[d]}, device_id_type=pl.DeviceIdType.MESH
        )
    loads = [
        pltpu.make_async_copy(src, dst, in_sem.at[i])
        for i, (src, dst) in enumerate(
            [(q_hbm, q_v), (k_hbm, k_v), (v_hbm, v_v), (c_hbm, c_v), (w_hbm, w_v)]
        )
    ]
    for load in loads:
        load.start()

    def remote(kind, d, src, dst):
        return pltpu.make_async_remote_copy(
            src_ref=src,
            dst_ref=dst,
            send_sem=send_sem.at[kind, d],
            recv_sem=recv_sem.at[kind, d],
            device_id={"ctx": peers[d]},
            device_id_type=pl.DeviceIdType.MESH,
        )

    row_id = lax.broadcasted_iota(jnp.int32, (rows, rows), 0)
    col_id = lax.broadcasted_iota(jnp.int32, (rows, rows), 1)
    order = (col_id == R * (row_id % per) + row_id // per).astype(F32).astype(BF16)
    left_row = lax.broadcasted_iota(jnp.int32, (1, LANES), 1) < DH

    for load in loads[:3]:
        load.wait()
    for c in range(n):
        cols = pl.ds(c * LANES, LANES)
        picker = order[c * group : (c + 1) * group, :]
        parts = []
        for ref in (q_v, k_v, v_v):
            picked = mm(picker, ref[:, cols], NN)
            parts.append(jnp.where(left_row, picked[:per], picked[per:]))
        parts.append(jnp.zeros_like(parts[0]))
        qkv_send[c] = jnp.concatenate(parts, axis=0).astype(BF16)
    loads[3].wait()
    for c in range(n):
        cols = pl.ds(c * LANES, LANES)
        cot_send[c] = mm(order, c_v[:, cols], NN).astype(BF16)
    qkv_recv[me] = qkv_send[me]
    cot_recv[me] = cot_send[me]

    pl.semaphore_wait(barrier, n - 1)
    qkv_copies = [remote(0, d, qkv_send.at[peers[d]], qkv_recv.at[me]) for d in range(1, n)]
    cot_copies = [remote(1, d, cot_send.at[peers[d]], cot_recv.at[me]) for d in range(1, n)]
    for copy in qkv_copies:
        copy.start()
    for copy in cot_copies:
        copy.start()
    loads[4].wait()

    for copy in qkv_copies:
        copy.wait_recv()
    got = qkv_recv[...].astype(F32)

    def taken(j):
        return got[:, j * per : (j + 1) * per, :].reshape(total, LANES)

    def split(x):
        zero = jnp.zeros_like(x)
        return jnp.concatenate(
            [jnp.where(left_row, x, zero), jnp.where(left_row, zero, x)], axis=0
        )

    def joined(x):
        return jnp.where(left_row, x[:total], x[total:])

    scale = DH ** (-0.5)
    q_two = split(taken(0)).astype(BF16)
    k_all = taken(1).astype(BF16)
    v_all = taken(2).astype(BF16)
    seg_rows = seg_devices * per
    q_seg = (lax.broadcasted_iota(jnp.int32, (2 * total, total), 0) % total) // seg_rows
    k_seg = lax.broadcasted_iota(jnp.int32, (2 * total, total), 1) // seg_rows
    same = q_seg == k_seg
    scores = jnp.where(same, mm(q_two, k_all, NT) * scale, -jnp.inf)
    raised = jnp.exp(scores - jnp.max(scores, axis=-1, keepdims=True))
    prob = raised / jnp.sum(raised, axis=-1, keepdims=True)
    prob_16 = prob.astype(BF16)
    attn = joined(mm(prob_16, v_all, NN)).astype(BF16)
    attn_recv[me] = attn
    attn_copies = [remote(2, d, attn_recv.at[me], attn_recv.at[me]) for d in range(1, n)]
    for copy in attn_copies:
        copy.start()

    for copy in cot_copies:
        copy.wait_recv()

    def cot_group(c):
        picked = cot_recv[:, pl.ds(pl.multiple_of(c * group, group), group), :]
        return picked.reshape(n * group, LANES)

    def tile(c):
        return pl.ds(pl.multiple_of(c * LANES, LANES), LANES)

    da_copies = []
    own_da = None
    for d in list(range(1, n)) + [0]:
        c = peers[d]
        both = mm(cot_group(c), w_v[:, tile(c)], NN).reshape(n, 2, per, LANES)
        share = jnp.where(left_row, both[:, 0], both[:, 1]).reshape(total, LANES)
        if d == 0:
            own_da = share
            continue
        da_send[d] = share.astype(BF16)
        copy = remote(3, d, da_send.at[d], da_recv.at[d])
        copy.start()
        da_copies.append(copy)

    for d in range(n):
        c = sources[d]
        if d:
            attn_copies[d - 1].wait_recv()
        packed = attn_recv[c].astype(F32).reshape(n, per, LANES)
        zero = jnp.zeros_like(packed)
        wide = jnp.stack([jnp.where(left_row, packed, zero), jnp.where(left_row, zero, packed)], axis=1)
        wide = wide.reshape(n * group, LANES).astype(BF16)
        attn2[d] = wide
        out = mm(wide, w_v[:, tile(c)], NT).astype(BF16)
        pr_send[:, pl.ds(pl.multiple_of(c * group, group), group), :] = out.reshape(n, group, LANES)
    keep_pr = pltpu.make_async_copy(pr_send.at[me], pr_recv.at[me], out_sem.at[0])
    keep_pr.start()
    pr_copies = [remote(4, d, pr_send.at[peers[d]], pr_recv.at[me]) for d in range(1, n)]
    for copy in pr_copies:
        copy.start()

    for copy in da_copies:
        copy.wait_recv()
    da = own_da
    for d in range(1, n):
        da = da + da_recv[d].astype(F32)
    da_two = split(da).astype(BF16)
    attn_two = split(attn.astype(F32))
    delta = jnp.sum(da_two.astype(F32) * attn_two, axis=-1, keepdims=True)
    d_score = (prob * (mm(da_two, v_all, NT) - delta)).astype(BF16)
    dq = joined(mm(d_score, k_all, NN)) * scale
    dk = mm(d_score, q_two, TN) * scale
    dv = mm(prob_16, da_two, TN)
    grads = [g.reshape(n, per, LANES) for g in (dq, dk, dv)]
    grads.append(jnp.zeros_like(grads[0]))
    dg_send[...] = jnp.concatenate(grads, axis=1).astype(BF16)
    keep_dg = pltpu.make_async_copy(dg_send.at[me], dg_recv.at[me], out_sem.at[1])
    keep_dg.start()
    dg_copies = [remote(5, d, dg_send.at[peers[d]], dg_recv.at[me]) for d in range(1, n)]
    for copy in dg_copies:
        copy.start()

    for d in range(n):
        c = sources[d]
        wg_out[:, tile(c)] = mm(cot_group(c), attn2[d], TN)
    keep_wg = pltpu.make_async_copy(wg_out, wg_any, out_sem.at[2])
    keep_wg.start()

    for copy in pr_copies + dg_copies:
        copy.wait_recv()
    for copy in qkv_copies + cot_copies + attn_copies + da_copies + pr_copies + dg_copies:
        copy.wait_send()
    for keep in (keep_pr, keep_dg, keep_wg):
        keep.wait()


def finish_kernel(
    n, rows,
    pr_any, dg_any, wg_any,
    proj_hbm, wg_hbm, dq_hbm, dk_hbm, dv_hbm,
    pr_v, dg_v, pr_out, dq_out, dk_out, dv_out, in_sem, out_sem,
):
    per = rows // R
    load_pr = pltpu.make_async_copy(pr_any, pr_v, in_sem.at[0])
    load_dg = pltpu.make_async_copy(dg_any, dg_v, in_sem.at[1])
    load_dg.start()
    load_pr.start()
    stores = [
        pltpu.make_async_copy(src, dst, out_sem.at[i])
        for i, (src, dst) in enumerate(
            [(wg_any, wg_hbm), (pr_out, proj_hbm), (dq_out, dq_hbm), (dk_out, dk_hbm), (dv_out, dv_hbm)]
        )
    ]
    stores[0].start()
    load_dg.wait()
    head = lax.broadcasted_iota(jnp.int32, (R, LANES), 0)
    lane_head = lax.broadcasted_iota(jnp.int32, (R, LANES), 1) // DH
    for j, out in enumerate((dq_out, dk_out, dv_out)):
        for c in range(n):
            block = dg_v[c].astype(F32)[j * per : (j + 1) * per]
            here = (lane_head + 2 * c == head)[None]
            spread_out = jnp.where(here, block[:, None, :], 0.0)
            out[:, c * LANES : (c + 1) * LANES] = spread_out.reshape(rows, LANES).astype(BF16)
        stores[2 + j].start()
    row_id = lax.broadcasted_iota(jnp.int32, (rows, rows), 0)
    col_id = lax.broadcasted_iota(jnp.int32, (rows, rows), 1)
    order = (row_id == R * (col_id % per) + col_id // per).astype(F32).astype(BF16)
    load_pr.wait()
    for c in range(n):
        pr_out[:, c * LANES : (c + 1) * LANES] = mm(order, pr_v[c], NN).astype(BF16)
    stores[1].start()
    for store in stores:
        store.wait()


def fused(queries, keys, values, cotangent, out_weight):
    n = lax.axis_size("ctx")
    rows = queries.shape[0]
    per = rows // R
    total = n * per
    full = (rows, D)
    square = (n, rows, LANES)
    compact = (n, 4 * per, LANES)
    packed = (n, total, LANES)
    anywhere = pl.BlockSpec(memory_space=pl.ANY)
    in_hbm = pl.BlockSpec(memory_space=pltpu.HBM)
    room = 60 * 1024 * 1024
    pieces = pl.pallas_call(
        functools.partial(fused_kernel, n, rows),
        out_shape=(
            jax.ShapeDtypeStruct(square, BF16),
            jax.ShapeDtypeStruct(compact, BF16),
            jax.ShapeDtypeStruct((D // n, D), F32),
        ),
        in_specs=[in_hbm] * 5,
        out_specs=[anywhere] * 3,
        scratch_shapes=[pltpu.VMEM(full, BF16)] * 4
        + [
            pltpu.VMEM((D // n, D), BF16),
            pltpu.VMEM(compact, BF16),
            pltpu.VMEM(compact, BF16),
            pltpu.VMEM(square, BF16),
            pltpu.VMEM(square, BF16),
            pltpu.VMEM(packed, BF16),
            pltpu.VMEM(packed, BF16),
            pltpu.VMEM(packed, BF16),
            pltpu.VMEM(square, BF16),
            pltpu.VMEM(compact, BF16),
            pltpu.VMEM((n, n * 2 * per, LANES), BF16),
            pltpu.VMEM((D // n, D), F32),
            pltpu.SemaphoreType.DMA((6, n)),
            pltpu.SemaphoreType.DMA((6, n)),
            pltpu.SemaphoreType.DMA((5,)),
            pltpu.SemaphoreType.DMA((3,)),
        ],
        compiler_params=pltpu.CompilerParams(
            collective_id=0, has_side_effects=True, vmem_limit_bytes=room
        ),
    )(queries, keys, values, cotangent, out_weight)
    return pl.pallas_call(
        functools.partial(finish_kernel, n, rows),
        out_shape=(
            jax.ShapeDtypeStruct(full, BF16),
            jax.ShapeDtypeStruct((D // n, D), F32),
            jax.ShapeDtypeStruct(full, BF16),
            jax.ShapeDtypeStruct(full, BF16),
            jax.ShapeDtypeStruct(full, BF16),
        ),
        in_specs=[anywhere] * 3,
        out_specs=[in_hbm] * 5,
        scratch_shapes=[pltpu.VMEM(square, BF16), pltpu.VMEM(compact, BF16)]
        + [pltpu.VMEM(full, BF16)] * 4
        + [pltpu.SemaphoreType.DMA((2,)), pltpu.SemaphoreType.DMA((5,))],
        compiler_params=pltpu.CompilerParams(vmem_limit_bytes=room),
    )(*pieces)


def solution(mesh):
    in_specs = (
        P(("dp", "ctx"), None),
        P(("dp", "ctx"), None),
        P(("dp", "ctx"), None),
        P(("dp", "ctx"), None),
        P("ctx", None),
    )
    out_specs = (
        P(("dp", "ctx"), None),
        P(("dp", "ctx"), None),
        P(("dp", "ctx"), None),
        P(("dp", "ctx"), None),
        P(("dp", "ctx"), None),
    )
    body = fused if fits(mesh) else shards
    return jax.shard_map(body, mesh=mesh, in_specs=in_specs, out_specs=out_specs, check_vma=False)
```

```python
import functools

import jax
import jax.numpy as jnp
from jax import lax
from jax.experimental import pallas as pl
from jax.experimental.pallas import tpu as pltpu
from jax.sharding import PartitionSpec as P

H = 16
DH = 64
R = 16


def partner_2(value, axis, apart):
    mask = 2**apart
    pairs = [(source, source ^ mask) for source in range(lax.axis_size(axis))]
    return lax.ppermute(value, axis, pairs)


def select_mask(dtype):
    residue = jnp.arange(R)[:, None]
    head_ids = jnp.arange(H)[None, :]
    return (head_ids % R == residue).astype(dtype)[:, :, None]


def sparse_rows(full_rows):
    reshaped = full_rows.reshape(full_rows.shape[0] // R, R, H, DH)
    return jnp.sum(reshaped * select_mask(full_rows.dtype), axis=1)


def dense_rows(sparse):
    placed = sparse[:, None, :, :] * select_mask(sparse.dtype)
    return placed.reshape(sparse.shape[0] * R, H * DH)


def spread(payload, swapper, bit_list, device_index):
    visited = []
    gathered = payload
    for bit_num in bit_list:
        partner = swapper(gathered, bit_num)
        upper_half = device_index // (1 << bit_num) % 2 == 1
        gathered = jnp.where(
            upper_half, jnp.stack([partner, gathered]), jnp.stack([gathered, partner])
        )
        visited.insert(0, bit_num)
    axis_order = [visited.index(bit_num) for bit_num in sorted(visited, reverse=True)]
    trailing = list(range(len(visited), gathered.ndim))
    gathered = jnp.transpose(gathered, axis_order + trailing)
    return gathered.reshape((-1,) + payload.shape[1:])


def shards(queries, keys, values, cotangent, out_weight):
    ctx_size = lax.axis_size("ctx")
    seg_devices = min(64, ctx_size // 2)
    seg_bits = seg_devices.bit_length() - 1
    device_index = lax.axis_index("ctx")
    bit_list = list(range(seg_bits))
    score_scale = DH ** (-0.5)
    q_sparse = sparse_rows(queries)
    k_sparse = sparse_rows(keys)
    v_sparse = sparse_rows(values)
    gathered = spread(
        jnp.stack([k_sparse, v_sparse], axis=1),
        lambda payload, bit_num: partner_2(payload, "ctx", bit_num),
        bit_list,
        device_index,
    )
    seg_keys = gathered[:, 0]
    seg_values = gathered[:, 1]
    full_weight = lax.all_gather(out_weight, "ctx", axis=0, tiled=True)
    scores = (
        jnp.einsum("qhd,khd->hqk", q_sparse, seg_keys, preferred_element_type=jnp.float32)
        * score_scale
    )
    row_top = jnp.max(scores, axis=-1, keepdims=True)
    log_total = row_top + jnp.log(jnp.sum(jnp.exp(scores - row_top), axis=-1, keepdims=True))
    probability = jnp.exp(scores - log_total)
    attn_sparse = jnp.einsum(
        "hqk,khd->qhd",
        probability.astype(jnp.bfloat16),
        seg_values,
        preferred_element_type=jnp.float32,
    ).astype(jnp.bfloat16)
    attention = dense_rows(attn_sparse)
    projected = lax.dot_general(
        attention, full_weight, (((1,), (1,)), ((), ())), preferred_element_type=jnp.float32
    ).astype(jnp.bfloat16)
    weight_grad = lax.psum_scatter(
        lax.dot_general(
            cotangent, attention, (((0,), (0,)), ((), ())), preferred_element_type=jnp.float32
        ),
        "ctx",
        scatter_dimension=0,
        tiled=True,
    )
    d_attention = jnp.dot(cotangent, full_weight, preferred_element_type=jnp.float32).astype(
        jnp.bfloat16
    )
    da_sparse = sparse_rows(d_attention)
    row_delta = jnp.sum(da_sparse.astype(jnp.float32) * attn_sparse.astype(jnp.float32), axis=-1)
    prob_grad = jnp.einsum(
        "qhd,khd->hqk", da_sparse, seg_values, preferred_element_type=jnp.float32
    )
    score_grad = (probability * (prob_grad - row_delta.T[:, :, None])).astype(jnp.bfloat16)
    query_part = (
        jnp.einsum("hqk,khd->qhd", score_grad, seg_keys, preferred_element_type=jnp.float32)
        * score_scale
    ).astype(jnp.bfloat16)
    row_stats = jnp.stack([log_total[:, :, 0].T, row_delta], axis=1)
    seg_stats = spread(
        row_stats,
        lambda payload, bit_num: partner_2(payload, "ctx", bit_num),
        bit_list,
        device_index,
    )
    paired = spread(
        jnp.stack([q_sparse, da_sparse], axis=1),
        lambda payload, bit_num: partner_2(payload, "ctx", bit_num),
        bit_list,
        device_index,
    )
    seg_queries = paired[:, 0]
    seg_cotangent = paired[:, 1]
    key_scores = (
        jnp.einsum("qhd,khd->hqk", seg_queries, k_sparse, preferred_element_type=jnp.float32)
        * score_scale
    )
    key_prob = jnp.exp(key_scores - seg_stats[:, 0].T[:, :, None])
    key_dgrad = jnp.einsum(
        "qhd,khd->hqk", seg_cotangent, v_sparse, preferred_element_type=jnp.float32
    )
    key_dscore = (key_prob * (key_dgrad - seg_stats[:, 1].T[:, :, None])).astype(jnp.bfloat16)
    key_part = (
        jnp.einsum("hqk,qhd->khd", key_dscore, seg_queries, preferred_element_type=jnp.float32)
        * score_scale
    ).astype(jnp.bfloat16)
    value_part = jnp.einsum(
        "hqk,qhd->khd",
        key_prob.astype(jnp.bfloat16),
        seg_cotangent,
        preferred_element_type=jnp.float32,
    ).astype(jnp.bfloat16)
    return (
        projected,
        weight_grad,
        dense_rows(query_part),
        dense_rows(key_part),
        dense_rows(value_part),
    )


LANES = 128
D = H * DH
F32 = jnp.float32
BF16 = jnp.bfloat16


def fits(mesh):
    return mesh.shape["ctx"] * LANES == D


def mm(a, b, dims):
    return lax.dot_general(a, b, (dims, ((), ())), preferred_element_type=F32)


NN = ((1,), (0,))
NT = ((1,), (1,))
TN = ((0,), (0,))


def fused_kernel(
    n, rows,
    q_hbm, k_hbm, v_hbm, c_hbm, w_hbm,
    pr_recv, dg_recv, wg_any,
    q_v, k_v, v_v, c_v, w_v,
    qkv_send, qkv_recv, cot_send, cot_recv, attn_recv, da_send, da_recv,
    pr_send, dg_send, attn2, wg_out,
    send_sem, recv_sem, in_sem, out_sem,
):
    per = rows // R
    group = 2 * per
    seg_devices = n // 2
    total = n * per
    me = lax.axis_index("ctx")
    peers = [lax.rem(me + d, n) for d in range(n)]
    sources = [lax.rem(me + n - d, n) for d in range(n)]

    barrier = pltpu.get_barrier_semaphore()
    for d in range(1, n):
        pl.semaphore_signal(
            barrier, inc=1, device_id={"ctx": peers[d]}, device_id_type=pl.DeviceIdType.MESH
        )
    loads = [
        pltpu.make_async_copy(src, dst, in_sem.at[i])
        for i, (src, dst) in enumerate(
            [(q_hbm, q_v), (k_hbm, k_v), (v_hbm, v_v), (c_hbm, c_v), (w_hbm, w_v)]
        )
    ]
    for load in loads:
        load.start()

    def remote(kind, d, src, dst):
        return pltpu.make_async_remote_copy(
            src_ref=src,
            dst_ref=dst,
            send_sem=send_sem.at[kind, d],
            recv_sem=recv_sem.at[kind, d],
            device_id={"ctx": peers[d]},
            device_id_type=pl.DeviceIdType.MESH,
        )

    row_id = lax.broadcasted_iota(jnp.int32, (rows, rows), 0)
    col_id = lax.broadcasted_iota(jnp.int32, (rows, rows), 1)
    order = (col_id == R * (row_id % per) + row_id // per).astype(F32).astype(BF16)
    left_row = lax.broadcasted_iota(jnp.int32, (1, LANES), 1) < DH

    for load in loads[:3]:
        load.wait()
    for c in range(n):
        cols = pl.ds(c * LANES, LANES)
        picker = order[c * group : (c + 1) * group, :]
        parts = []
        for ref in (q_v, k_v, v_v):
            picked = mm(picker, ref[:, cols], NN)
            parts.append(jnp.where(left_row, picked[:per], picked[per:]))
        parts.append(jnp.zeros_like(parts[0]))
        qkv_send[c] = jnp.concatenate(parts, axis=0).astype(BF16)
    loads[3].wait()
    for c in range(n):
        cols = pl.ds(c * LANES, LANES)
        cot_send[c] = mm(order, c_v[:, cols], NN).astype(BF16)
    qkv_recv[me] = qkv_send[me]
    cot_recv[me] = cot_send[me]

    pl.semaphore_wait(barrier, n - 1)
    qkv_copies = [remote(0, d, qkv_send.at[peers[d]], qkv_recv.at[me]) for d in range(1, n)]
    cot_copies = [remote(1, d, cot_send.at[peers[d]], cot_recv.at[me]) for d in range(1, n)]
    for copy in qkv_copies:
        copy.start()
    for copy in cot_copies:
        copy.start()
    loads[4].wait()

    for copy in qkv_copies:
        copy.wait_recv()
    got = qkv_recv[...].astype(F32)

    def taken(j):
        return got[:, j * per : (j + 1) * per, :].reshape(total, LANES)

    def split(x):
        zero = jnp.zeros_like(x)
        return jnp.concatenate(
            [jnp.where(left_row, x, zero), jnp.where(left_row, zero, x)], axis=0
        )

    def joined(x):
        return jnp.where(left_row, x[:total], x[total:])

    scale = DH ** (-0.5)
    q_two = split(taken(0)).astype(BF16)
    k_all = taken(1).astype(BF16)
    v_all = taken(2).astype(BF16)
    seg_rows = seg_devices * per
    q_seg = (lax.broadcasted_iota(jnp.int32, (2 * total, total), 0) % total) // seg_rows
    k_seg = lax.broadcasted_iota(jnp.int32, (2 * total, total), 1) // seg_rows
    same = q_seg == k_seg
    scores = jnp.where(same, mm(q_two, k_all, NT) * scale, -jnp.inf)
    raised = jnp.exp(scores - jnp.max(scores, axis=-1, keepdims=True))
    prob = raised / jnp.sum(raised, axis=-1, keepdims=True)
    prob_16 = prob.astype(BF16)
    attn = joined(mm(prob_16, v_all, NN)).astype(BF16)
    attn_recv[me] = attn
    attn_copies = [remote(2, d, attn_recv.at[me], attn_recv.at[me]) for d in range(1, n)]
    for copy in attn_copies:
        copy.start()

    for copy in cot_copies:
        copy.wait_recv()

    def cot_group(c):
        picked = cot_recv[:, pl.ds(pl.multiple_of(c * group, group), group), :]
        return picked.reshape(n * group, LANES)

    def tile(c):
        return pl.ds(pl.multiple_of(c * LANES, LANES), LANES)

    da_copies = []
    own_da = None
    for d in list(range(1, n)) + [0]:
        c = peers[d]
        both = mm(cot_group(c), w_v[:, tile(c)], NN).reshape(n, 2, per, LANES)
        share = jnp.where(left_row, both[:, 0], both[:, 1]).reshape(total, LANES)
        if d == 0:
            own_da = share
            continue
        da_send[d] = share.astype(BF16)
        copy = remote(3, d, da_send.at[d], da_recv.at[d])
        copy.start()
        da_copies.append(copy)

    for d in range(n):
        c = sources[d]
        if d:
            attn_copies[d - 1].wait_recv()
        packed = attn_recv[c].astype(F32).reshape(n, per, LANES)
        zero = jnp.zeros_like(packed)
        wide = jnp.stack([jnp.where(left_row, packed, zero), jnp.where(left_row, zero, packed)], axis=1)
        wide = wide.reshape(n * group, LANES).astype(BF16)
        attn2[d] = wide
        out = mm(wide, w_v[:, tile(c)], NT).astype(BF16)
        pr_send[:, pl.ds(pl.multiple_of(c * group, group), group), :] = out.reshape(n, group, LANES)
    keep_pr = pltpu.make_async_copy(pr_send.at[me], pr_recv.at[me], out_sem.at[0])
    keep_pr.start()
    pr_copies = [remote(4, d, pr_send.at[peers[d]], pr_recv.at[me]) for d in range(1, n)]
    for copy in pr_copies:
        copy.start()

    for copy in da_copies:
        copy.wait_recv()
    da = own_da
    for d in range(1, n):
        da = da + da_recv[d].astype(F32)
    da_two = split(da).astype(BF16)
    attn_two = split(attn.astype(F32))
    delta = jnp.sum(da_two.astype(F32) * attn_two, axis=-1, keepdims=True)
    d_score = (prob * (mm(da_two, v_all, NT) - delta)).astype(BF16)
    dq = joined(mm(d_score, k_all, NN)) * scale
    dk = mm(d_score, q_two, TN) * scale
    dv = mm(prob_16, da_two, TN)
    grads = [g.reshape(n, per, LANES) for g in (dq, dk, dv)]
    grads.append(jnp.zeros_like(grads[0]))
    dg_send[...] = jnp.concatenate(grads, axis=1).astype(BF16)
    keep_dg = pltpu.make_async_copy(dg_send.at[me], dg_recv.at[me], out_sem.at[1])
    keep_dg.start()
    dg_copies = [remote(5, d, dg_send.at[peers[d]], dg_recv.at[me]) for d in range(1, n)]
    for copy in dg_copies:
        copy.start()

    for d in range(n):
        c = sources[d]
        wg_out[:, tile(c)] = mm(cot_group(c), attn2[d], TN)
    keep_wg = pltpu.make_async_copy(wg_out, wg_any, out_sem.at[2])
    keep_wg.start()

    for copy in pr_copies + dg_copies:
        copy.wait_recv()
    for copy in qkv_copies + cot_copies + attn_copies + da_copies + pr_copies + dg_copies:
        copy.wait_send()
    for keep in (keep_pr, keep_dg, keep_wg):
        keep.wait()


def finish_kernel(
    n, rows,
    pr_any, dg_any, wg_any,
    proj_hbm, wg_hbm, dq_hbm, dk_hbm, dv_hbm,
    pr_v, dg_v, wg_v, pr_out, dq_out, dk_out, dv_out, in_sem, out_sem,
):
    per = rows // R
    load_pr = pltpu.make_async_copy(pr_any, pr_v, in_sem.at[0])
    load_dg = pltpu.make_async_copy(dg_any, dg_v, in_sem.at[1])
    load_wg = pltpu.make_async_copy(wg_any, wg_v, in_sem.at[2])
    load_dg.start()
    load_pr.start()
    load_wg.start()
    stores = [
        pltpu.make_async_copy(src, dst, out_sem.at[i])
        for i, (src, dst) in enumerate(
            [(wg_v, wg_hbm), (pr_out, proj_hbm), (dq_out, dq_hbm), (dk_out, dk_hbm), (dv_out, dv_hbm)]
        )
    ]
    load_dg.wait()
    head = lax.broadcasted_iota(jnp.int32, (R, LANES), 0)
    lane_head = lax.broadcasted_iota(jnp.int32, (R, LANES), 1) // DH
    for j, out in enumerate((dq_out, dk_out, dv_out)):
        for c in range(n):
            block = dg_v[c].astype(F32)[j * per : (j + 1) * per]
            here = (lane_head + 2 * c == head)[None]
            spread_out = jnp.where(here, block[:, None, :], 0.0)
            out[:, c * LANES : (c + 1) * LANES] = spread_out.reshape(rows, LANES).astype(BF16)
        stores[2 + j].start()
    row_id = lax.broadcasted_iota(jnp.int32, (rows, rows), 0)
    col_id = lax.broadcasted_iota(jnp.int32, (rows, rows), 1)
    order = (row_id == R * (col_id % per) + col_id // per).astype(F32).astype(BF16)
    load_wg.wait()
    stores[0].start()
    load_pr.wait()
    for c in range(n):
        pr_out[:, c * LANES : (c + 1) * LANES] = mm(order, pr_v[c], NN).astype(BF16)
    stores[1].start()
    for store in stores:
        store.wait()


def fused(queries, keys, values, cotangent, out_weight):
    n = lax.axis_size("ctx")
    rows = queries.shape[0]
    per = rows // R
    total = n * per
    full = (rows, D)
    square = (n, rows, LANES)
    compact = (n, 4 * per, LANES)
    packed = (n, total, LANES)
    anywhere = pl.BlockSpec(memory_space=pl.ANY)
    in_hbm = pl.BlockSpec(memory_space=pltpu.HBM)
    room = 60 * 1024 * 1024
    pieces = pl.pallas_call(
        functools.partial(fused_kernel, n, rows),
        out_shape=(
            jax.ShapeDtypeStruct(square, BF16),
            jax.ShapeDtypeStruct(compact, BF16),
            jax.ShapeDtypeStruct((D // n, D), F32),
        ),
        in_specs=[in_hbm] * 5,
        out_specs=[anywhere] * 3,
        scratch_shapes=[pltpu.VMEM(full, BF16)] * 4
        + [
            pltpu.VMEM((D // n, D), BF16),
            pltpu.VMEM(compact, BF16),
            pltpu.VMEM(compact, BF16),
            pltpu.VMEM(square, BF16),
            pltpu.VMEM(square, BF16),
            pltpu.VMEM(packed, BF16),
            pltpu.VMEM(packed, BF16),
            pltpu.VMEM(packed, BF16),
            pltpu.VMEM(square, BF16),
            pltpu.VMEM(compact, BF16),
            pltpu.VMEM((n, n * 2 * per, LANES), BF16),
            pltpu.VMEM((D // n, D), F32),
            pltpu.SemaphoreType.DMA((6, n)),
            pltpu.SemaphoreType.DMA((6, n)),
            pltpu.SemaphoreType.DMA((5,)),
            pltpu.SemaphoreType.DMA((3,)),
        ],
        compiler_params=pltpu.CompilerParams(
            collective_id=0, has_side_effects=True, vmem_limit_bytes=room
        ),
    )(queries, keys, values, cotangent, out_weight)
    return pl.pallas_call(
        functools.partial(finish_kernel, n, rows),
        out_shape=(
            jax.ShapeDtypeStruct(full, BF16),
            jax.ShapeDtypeStruct((D // n, D), F32),
            jax.ShapeDtypeStruct(full, BF16),
            jax.ShapeDtypeStruct(full, BF16),
            jax.ShapeDtypeStruct(full, BF16),
        ),
        in_specs=[anywhere] * 3,
        out_specs=[in_hbm] * 5,
        scratch_shapes=[pltpu.VMEM(square, BF16), pltpu.VMEM(compact, BF16), pltpu.VMEM((D // n, D), F32)]
        + [pltpu.VMEM(full, BF16)] * 4
        + [pltpu.SemaphoreType.DMA((3,)), pltpu.SemaphoreType.DMA((5,))],
        compiler_params=pltpu.CompilerParams(vmem_limit_bytes=room),
    )(*pieces)


def solution(mesh):
    in_specs = (
        P(("dp", "ctx"), None),
        P(("dp", "ctx"), None),
        P(("dp", "ctx"), None),
        P(("dp", "ctx"), None),
        P("ctx", None),
    )
    out_specs = (
        P(("dp", "ctx"), None),
        P(("dp", "ctx"), None),
        P(("dp", "ctx"), None),
        P(("dp", "ctx"), None),
        P(("dp", "ctx"), None),
    )
    body = fused if fits(mesh) else shards
    return jax.shard_map(body, mesh=mesh, in_specs=in_specs, out_specs=out_specs, check_vma=False)
```

```python
import functools

import jax
import jax.numpy as jnp
from jax import lax
from jax.experimental import pallas as pl
from jax.experimental.pallas import tpu as pltpu
from jax.sharding import PartitionSpec as P

H = 16
DH = 64
R = 16


def partner_2(value, axis, apart):
    mask = 2**apart
    pairs = [(source, source ^ mask) for source in range(lax.axis_size(axis))]
    return lax.ppermute(value, axis, pairs)


def select_mask(dtype):
    residue = jnp.arange(R)[:, None]
    head_ids = jnp.arange(H)[None, :]
    return (head_ids % R == residue).astype(dtype)[:, :, None]


def sparse_rows(full_rows):
    reshaped = full_rows.reshape(full_rows.shape[0] // R, R, H, DH)
    return jnp.sum(reshaped * select_mask(full_rows.dtype), axis=1)


def dense_rows(sparse):
    placed = sparse[:, None, :, :] * select_mask(sparse.dtype)
    return placed.reshape(sparse.shape[0] * R, H * DH)


def spread(payload, swapper, bit_list, device_index):
    visited = []
    gathered = payload
    for bit_num in bit_list:
        partner = swapper(gathered, bit_num)
        upper_half = device_index // (1 << bit_num) % 2 == 1
        gathered = jnp.where(
            upper_half, jnp.stack([partner, gathered]), jnp.stack([gathered, partner])
        )
        visited.insert(0, bit_num)
    axis_order = [visited.index(bit_num) for bit_num in sorted(visited, reverse=True)]
    trailing = list(range(len(visited), gathered.ndim))
    gathered = jnp.transpose(gathered, axis_order + trailing)
    return gathered.reshape((-1,) + payload.shape[1:])


def shards(queries, keys, values, cotangent, out_weight):
    ctx_size = lax.axis_size("ctx")
    seg_devices = min(64, ctx_size // 2)
    seg_bits = seg_devices.bit_length() - 1
    device_index = lax.axis_index("ctx")
    bit_list = list(range(seg_bits))
    score_scale = DH ** (-0.5)
    q_sparse = sparse_rows(queries)
    k_sparse = sparse_rows(keys)
    v_sparse = sparse_rows(values)
    gathered = spread(
        jnp.stack([k_sparse, v_sparse], axis=1),
        lambda payload, bit_num: partner_2(payload, "ctx", bit_num),
        bit_list,
        device_index,
    )
    seg_keys = gathered[:, 0]
    seg_values = gathered[:, 1]
    full_weight = lax.all_gather(out_weight, "ctx", axis=0, tiled=True)
    scores = (
        jnp.einsum("qhd,khd->hqk", q_sparse, seg_keys, preferred_element_type=jnp.float32)
        * score_scale
    )
    row_top = jnp.max(scores, axis=-1, keepdims=True)
    log_total = row_top + jnp.log(jnp.sum(jnp.exp(scores - row_top), axis=-1, keepdims=True))
    probability = jnp.exp(scores - log_total)
    attn_sparse = jnp.einsum(
        "hqk,khd->qhd",
        probability.astype(jnp.bfloat16),
        seg_values,
        preferred_element_type=jnp.float32,
    ).astype(jnp.bfloat16)
    attention = dense_rows(attn_sparse)
    projected = lax.dot_general(
        attention, full_weight, (((1,), (1,)), ((), ())), preferred_element_type=jnp.float32
    ).astype(jnp.bfloat16)
    weight_grad = lax.psum_scatter(
        lax.dot_general(
            cotangent, attention, (((0,), (0,)), ((), ())), preferred_element_type=jnp.float32
        ),
        "ctx",
        scatter_dimension=0,
        tiled=True,
    )
    d_attention = jnp.dot(cotangent, full_weight, preferred_element_type=jnp.float32).astype(
        jnp.bfloat16
    )
    da_sparse = sparse_rows(d_attention)
    row_delta = jnp.sum(da_sparse.astype(jnp.float32) * attn_sparse.astype(jnp.float32), axis=-1)
    prob_grad = jnp.einsum(
        "qhd,khd->hqk", da_sparse, seg_values, preferred_element_type=jnp.float32
    )
    score_grad = (probability * (prob_grad - row_delta.T[:, :, None])).astype(jnp.bfloat16)
    query_part = (
        jnp.einsum("hqk,khd->qhd", score_grad, seg_keys, preferred_element_type=jnp.float32)
        * score_scale
    ).astype(jnp.bfloat16)
    row_stats = jnp.stack([log_total[:, :, 0].T, row_delta], axis=1)
    seg_stats = spread(
        row_stats,
        lambda payload, bit_num: partner_2(payload, "ctx", bit_num),
        bit_list,
        device_index,
    )
    paired = spread(
        jnp.stack([q_sparse, da_sparse], axis=1),
        lambda payload, bit_num: partner_2(payload, "ctx", bit_num),
        bit_list,
        device_index,
    )
    seg_queries = paired[:, 0]
    seg_cotangent = paired[:, 1]
    key_scores = (
        jnp.einsum("qhd,khd->hqk", seg_queries, k_sparse, preferred_element_type=jnp.float32)
        * score_scale
    )
    key_prob = jnp.exp(key_scores - seg_stats[:, 0].T[:, :, None])
    key_dgrad = jnp.einsum(
        "qhd,khd->hqk", seg_cotangent, v_sparse, preferred_element_type=jnp.float32
    )
    key_dscore = (key_prob * (key_dgrad - seg_stats[:, 1].T[:, :, None])).astype(jnp.bfloat16)
    key_part = (
        jnp.einsum("hqk,qhd->khd", key_dscore, seg_queries, preferred_element_type=jnp.float32)
        * score_scale
    ).astype(jnp.bfloat16)
    value_part = jnp.einsum(
        "hqk,qhd->khd",
        key_prob.astype(jnp.bfloat16),
        seg_cotangent,
        preferred_element_type=jnp.float32,
    ).astype(jnp.bfloat16)
    return (
        projected,
        weight_grad,
        dense_rows(query_part),
        dense_rows(key_part),
        dense_rows(value_part),
    )


LANES = 128
D = H * DH
F32 = jnp.float32
BF16 = jnp.bfloat16


def fits(mesh):
    return mesh.shape["ctx"] * LANES == D


def mm(a, b, dims):
    return lax.dot_general(a, b, (dims, ((), ())), preferred_element_type=F32)


NN = ((1,), (0,))
NT = ((1,), (1,))
TN = ((0,), (0,))


def fused_kernel(
    n, rows,
    q_hbm, k_hbm, v_hbm, c_hbm, w_hbm,
    pr_recv, dg_recv, wg_any,
    q_v, k_v, v_v, c_v, w_v,
    qkv_send, qkv_recv, cot_send, cot_recv, attn_recv, da_send, da_recv, da_mate, da_from_mate,
    pr_send, dg_send, attn2, wg_out,
    send_sem, recv_sem, in_sem, out_sem,
):
    per = rows // R
    group = 2 * per
    seg_devices = n // 2
    total = n * per
    me = lax.axis_index("ctx")
    peers = [lax.rem(me + d, n) for d in range(n)]
    sources = [lax.rem(me + n - d, n) for d in range(n)]
    mate = me + 1 - 2 * lax.rem(me, 2)
    far_first = sorted(range(1, n), key=lambda d: abs(d - n // 2))

    barrier = pltpu.get_barrier_semaphore()
    for d in range(1, n):
        pl.semaphore_signal(
            barrier, inc=1, device_id={"ctx": peers[d]}, device_id_type=pl.DeviceIdType.MESH
        )
    loads = [
        pltpu.make_async_copy(src, dst, in_sem.at[i])
        for i, (src, dst) in enumerate(
            [(q_hbm, q_v), (k_hbm, k_v), (v_hbm, v_v), (c_hbm, c_v), (w_hbm, w_v)]
        )
    ]
    for load in loads:
        load.start()

    def remote(kind, d, src, dst, to=None):
        return pltpu.make_async_remote_copy(
            src_ref=src,
            dst_ref=dst,
            send_sem=send_sem.at[kind, d],
            recv_sem=recv_sem.at[kind, d],
            device_id={"ctx": peers[d] if to is None else to},
            device_id_type=pl.DeviceIdType.MESH,
        )

    row_id = lax.broadcasted_iota(jnp.int32, (rows, rows), 0)
    col_id = lax.broadcasted_iota(jnp.int32, (rows, rows), 1)
    order = (col_id == R * (row_id % per) + row_id // per).astype(F32).astype(BF16)
    left_row = lax.broadcasted_iota(jnp.int32, (1, LANES), 1) < DH

    for load in loads[:3]:
        load.wait()
    for c in range(n):
        cols = pl.ds(c * LANES, LANES)
        picker = order[c * group : (c + 1) * group, :]
        parts = []
        for ref in (q_v, k_v, v_v):
            picked = mm(picker, ref[:, cols], NN)
            parts.append(jnp.where(left_row, picked[:per], picked[per:]))
        parts.append(jnp.zeros_like(parts[0]))
        qkv_send[c] = jnp.concatenate(parts, axis=0).astype(BF16)
    qkv_recv[me] = qkv_send[me]
    pl.semaphore_wait(barrier, n - 1)
    qkv_copies = [remote(0, d, qkv_send.at[peers[d]], qkv_recv.at[me]) for d in far_first]
    for copy in qkv_copies:
        copy.start()

    def tile(c):
        return pl.ds(pl.multiple_of(c * LANES, LANES), LANES)

    loads[3].wait()
    cot_copies = []
    for d in far_first:
        cot_send[d] = mm(order, c_v[:, tile(peers[d])], NN).astype(BF16)
        copy = remote(1, d, cot_send.at[d], cot_recv.at[me])
        copy.start()
        cot_copies.append(copy)
    cot_recv[me] = mm(order, c_v[:, tile(me)], NN).astype(BF16)
    loads[4].wait()

    for copy in qkv_copies:
        copy.wait_recv()
    got = qkv_recv[...].astype(F32)

    def taken(j):
        return got[:, j * per : (j + 1) * per, :].reshape(total, LANES)

    def split(x):
        zero = jnp.zeros_like(x)
        return jnp.concatenate(
            [jnp.where(left_row, x, zero), jnp.where(left_row, zero, x)], axis=0
        )

    def joined(x):
        return jnp.where(left_row, x[:total], x[total:])

    scale = DH ** (-0.5)
    q_two = split(taken(0)).astype(BF16)
    k_all = taken(1).astype(BF16)
    v_all = taken(2).astype(BF16)
    seg_rows = seg_devices * per
    q_seg = (lax.broadcasted_iota(jnp.int32, (2 * total, total), 0) % total) // seg_rows
    k_seg = lax.broadcasted_iota(jnp.int32, (2 * total, total), 1) // seg_rows
    same = q_seg == k_seg
    scores = jnp.where(same, mm(q_two, k_all, NT) * scale, -jnp.inf)
    raised = jnp.exp(scores - jnp.max(scores, axis=-1, keepdims=True))
    prob = raised / jnp.sum(raised, axis=-1, keepdims=True)
    prob_16 = prob.astype(BF16)
    attn = joined(mm(prob_16, v_all, NN)).astype(BF16)
    attn_recv[me] = attn
    across = [remote(2, d, attn_recv.at[me], attn_recv.at[me]) for d in range(2, n, 2)]
    to_mate = remote(2, 1, attn_recv.at[me], attn_recv.at[me], mate)
    for copy in across + [to_mate]:
        copy.start()
    passed = []
    for i, d in enumerate(range(2, n, 2)):
        across[i].wait_recv()
        c = sources[d]
        copy = remote(2, d + 1, attn_recv.at[c], attn_recv.at[c], mate)
        copy.start()
        passed.append(copy)
    attn_copies = across + [to_mate] + passed

    for copy in cot_copies:
        copy.wait_recv()

    def cot_group(c):
        picked = cot_recv[:, pl.ds(pl.multiple_of(c * group, group), group), :]
        return picked.reshape(n * group, LANES)

    def da_share(c):
        both = mm(cot_group(c), w_v[:, tile(c)], NN).reshape(n, 2, per, LANES)
        return jnp.where(left_row, both[:, 0], both[:, 1]).reshape(total, LANES)

    chips = n // 2
    for t in range(chips):
        da_mate[t] = da_share(lax.rem(mate + 2 * t, n)).astype(BF16)
    mate_copy = remote(3, 1, da_mate, da_from_mate, mate)
    mate_copy.start()
    shares = [da_share(peers[2 * t]) for t in range(chips)]
    mate_copy.wait_recv()
    da_copies = []
    for t in range(1, chips):
        da_send[t] = (shares[t] + da_from_mate[t].astype(F32)).astype(BF16)
        copy = remote(3, 2 * t, da_send.at[t], da_recv.at[t])
        copy.start()
        da_copies.append(copy)
    own_da = shares[0] + da_from_mate[0].astype(F32)

    pairs = [sources[d] for d in range(0, n, 2)] + [lax.rem(mate + n - d, n) for d in range(0, n, 2)]
    for d, c in enumerate(pairs):
        if d == chips:
            to_mate.wait_recv()
        elif d > chips:
            passed[d - chips - 1].wait_recv()
        packed = attn_recv[c].astype(F32).reshape(n, per, LANES)
        zero = jnp.zeros_like(packed)
        wide = jnp.stack([jnp.where(left_row, packed, zero), jnp.where(left_row, zero, packed)], axis=1)
        wide = wide.reshape(n * group, LANES).astype(BF16)
        attn2[d] = wide
        out = mm(wide, w_v[:, tile(c)], NT).astype(BF16)
        pr_send[:, pl.ds(pl.multiple_of(c * group, group), group), :] = out.reshape(n, group, LANES)
    keep_pr = pltpu.make_async_copy(pr_send.at[me], pr_recv.at[me], out_sem.at[0])
    keep_pr.start()
    pr_copies = [remote(4, d, pr_send.at[peers[d]], pr_recv.at[me]) for d in far_first]
    for copy in pr_copies:
        copy.start()

    for copy in da_copies:
        copy.wait_recv()
    da = own_da
    for t in range(1, chips):
        da = da + da_recv[t].astype(F32)
    da_two = split(da).astype(BF16)
    attn_two = split(attn.astype(F32))
    delta = jnp.sum(da_two.astype(F32) * attn_two, axis=-1, keepdims=True)
    d_score = (prob * (mm(da_two, v_all, NT) - delta)).astype(BF16)
    dq = joined(mm(d_score, k_all, NN)) * scale
    dk = mm(d_score, q_two, TN) * scale
    dv = mm(prob_16, da_two, TN)
    grads = [g.reshape(n, per, LANES) for g in (dq, dk, dv)]
    grads.append(jnp.zeros_like(grads[0]))
    dg_send[...] = jnp.concatenate(grads, axis=1).astype(BF16)
    keep_dg = pltpu.make_async_copy(dg_send.at[me], dg_recv.at[me], out_sem.at[1])
    keep_dg.start()
    dg_copies = [remote(5, d, dg_send.at[peers[d]], dg_recv.at[me]) for d in range(1, n)]
    for copy in dg_copies:
        copy.start()

    for d, c in enumerate(pairs):
        wg_out[:, tile(c)] = mm(cot_group(c), attn2[d], TN)
    keep_wg = pltpu.make_async_copy(wg_out, wg_any, out_sem.at[2])
    keep_wg.start()

    for copy in pr_copies + dg_copies:
        copy.wait_recv()
    for copy in qkv_copies + cot_copies + attn_copies + [mate_copy] + da_copies + pr_copies + dg_copies:
        copy.wait_send()
    for keep in (keep_pr, keep_dg, keep_wg):
        keep.wait()


def finish_kernel(
    n, rows,
    pr_any, dg_any, wg_any,
    proj_hbm, wg_hbm, dq_hbm, dk_hbm, dv_hbm,
    pr_v, dg_v, wg_v, pr_out, dq_out, dk_out, dv_out, in_sem, out_sem,
):
    per = rows // R
    load_pr = pltpu.make_async_copy(pr_any, pr_v, in_sem.at[0])
    load_dg = pltpu.make_async_copy(dg_any, dg_v, in_sem.at[1])
    load_wg = pltpu.make_async_copy(wg_any, wg_v, in_sem.at[2])
    load_dg.start()
    load_pr.start()
    load_wg.start()
    stores = [
        pltpu.make_async_copy(src, dst, out_sem.at[i])
        for i, (src, dst) in enumerate(
            [(wg_v, wg_hbm), (pr_out, proj_hbm), (dq_out, dq_hbm), (dk_out, dk_hbm), (dv_out, dv_hbm)]
        )
    ]
    load_dg.wait()
    head = lax.broadcasted_iota(jnp.int32, (R, LANES), 0)
    lane_head = lax.broadcasted_iota(jnp.int32, (R, LANES), 1) // DH
    for j, out in enumerate((dq_out, dk_out, dv_out)):
        for c in range(n):
            block = dg_v[c].astype(F32)[j * per : (j + 1) * per]
            here = (lane_head + 2 * c == head)[None]
            spread_out = jnp.where(here, block[:, None, :], 0.0)
            out[:, c * LANES : (c + 1) * LANES] = spread_out.reshape(rows, LANES).astype(BF16)
        stores[2 + j].start()
    row_id = lax.broadcasted_iota(jnp.int32, (rows, rows), 0)
    col_id = lax.broadcasted_iota(jnp.int32, (rows, rows), 1)
    order = (row_id == R * (col_id % per) + col_id // per).astype(F32).astype(BF16)
    load_wg.wait()
    stores[0].start()
    load_pr.wait()
    for c in range(n):
        pr_out[:, c * LANES : (c + 1) * LANES] = mm(order, pr_v[c], NN).astype(BF16)
    stores[1].start()
    for store in stores:
        store.wait()


def fused(queries, keys, values, cotangent, out_weight):
    n = lax.axis_size("ctx")
    rows = queries.shape[0]
    per = rows // R
    total = n * per
    full = (rows, D)
    square = (n, rows, LANES)
    compact = (n, 4 * per, LANES)
    packed = (n, total, LANES)
    half = (n // 2, total, LANES)
    anywhere = pl.BlockSpec(memory_space=pl.ANY)
    in_hbm = pl.BlockSpec(memory_space=pltpu.HBM)
    room = 60 * 1024 * 1024
    pieces = pl.pallas_call(
        functools.partial(fused_kernel, n, rows),
        out_shape=(
            jax.ShapeDtypeStruct(square, BF16),
            jax.ShapeDtypeStruct(compact, BF16),
            jax.ShapeDtypeStruct((D // n, D), F32),
        ),
        in_specs=[in_hbm] * 5,
        out_specs=[anywhere] * 3,
        scratch_shapes=[pltpu.VMEM(full, BF16)] * 4
        + [
            pltpu.VMEM((D // n, D), BF16),
            pltpu.VMEM(compact, BF16),
            pltpu.VMEM(compact, BF16),
            pltpu.VMEM(square, BF16),
            pltpu.VMEM(square, BF16),
            pltpu.VMEM(packed, BF16),
            pltpu.VMEM(half, BF16),
            pltpu.VMEM(half, BF16),
            pltpu.VMEM(half, BF16),
            pltpu.VMEM(half, BF16),
            pltpu.VMEM(square, BF16),
            pltpu.VMEM(compact, BF16),
            pltpu.VMEM((n, n * 2 * per, LANES), BF16),
            pltpu.VMEM((D // n, D), F32),
            pltpu.SemaphoreType.DMA((6, n)),
            pltpu.SemaphoreType.DMA((6, n)),
            pltpu.SemaphoreType.DMA((5,)),
            pltpu.SemaphoreType.DMA((3,)),
        ],
        compiler_params=pltpu.CompilerParams(
            collective_id=0, has_side_effects=True, vmem_limit_bytes=room
        ),
    )(queries, keys, values, cotangent, out_weight)
    return pl.pallas_call(
        functools.partial(finish_kernel, n, rows),
        out_shape=(
            jax.ShapeDtypeStruct(full, BF16),
            jax.ShapeDtypeStruct((D // n, D), F32),
            jax.ShapeDtypeStruct(full, BF16),
            jax.ShapeDtypeStruct(full, BF16),
            jax.ShapeDtypeStruct(full, BF16),
        ),
        in_specs=[anywhere] * 3,
        out_specs=[in_hbm] * 5,
        scratch_shapes=[pltpu.VMEM(square, BF16), pltpu.VMEM(compact, BF16), pltpu.VMEM((D // n, D), F32)]
        + [pltpu.VMEM(full, BF16)] * 4
        + [pltpu.SemaphoreType.DMA((3,)), pltpu.SemaphoreType.DMA((5,))],
        compiler_params=pltpu.CompilerParams(vmem_limit_bytes=room),
    )(*pieces)


def solution(mesh):
    in_specs = (
        P(("dp", "ctx"), None),
        P(("dp", "ctx"), None),
        P(("dp", "ctx"), None),
        P(("dp", "ctx"), None),
        P("ctx", None),
    )
    out_specs = (
        P(("dp", "ctx"), None),
        P(("dp", "ctx"), None),
        P(("dp", "ctx"), None),
        P(("dp", "ctx"), None),
        P(("dp", "ctx"), None),
    )
    body = fused if fits(mesh) else shards
    return jax.shard_map(body, mesh=mesh, in_specs=in_specs, out_specs=out_specs, check_vma=False)
```

```python
import functools

import jax
import jax.numpy as jnp
from jax import lax
from jax.experimental import pallas as pl
from jax.experimental.pallas import tpu as pltpu
from jax.sharding import PartitionSpec as P

H = 16
DH = 64
R = 16


def partner_2(value, axis, apart):
    mask = 2**apart
    pairs = [(source, source ^ mask) for source in range(lax.axis_size(axis))]
    return lax.ppermute(value, axis, pairs)


def select_mask(dtype):
    residue = jnp.arange(R)[:, None]
    head_ids = jnp.arange(H)[None, :]
    return (head_ids % R == residue).astype(dtype)[:, :, None]


def sparse_rows(full_rows):
    reshaped = full_rows.reshape(full_rows.shape[0] // R, R, H, DH)
    return jnp.sum(reshaped * select_mask(full_rows.dtype), axis=1)


def dense_rows(sparse):
    placed = sparse[:, None, :, :] * select_mask(sparse.dtype)
    return placed.reshape(sparse.shape[0] * R, H * DH)


def spread(payload, swapper, bit_list, device_index):
    visited = []
    gathered = payload
    for bit_num in bit_list:
        partner = swapper(gathered, bit_num)
        upper_half = device_index // (1 << bit_num) % 2 == 1
        gathered = jnp.where(
            upper_half, jnp.stack([partner, gathered]), jnp.stack([gathered, partner])
        )
        visited.insert(0, bit_num)
    axis_order = [visited.index(bit_num) for bit_num in sorted(visited, reverse=True)]
    trailing = list(range(len(visited), gathered.ndim))
    gathered = jnp.transpose(gathered, axis_order + trailing)
    return gathered.reshape((-1,) + payload.shape[1:])


def shards(queries, keys, values, cotangent, out_weight):
    ctx_size = lax.axis_size("ctx")
    seg_devices = min(64, ctx_size // 2)
    seg_bits = seg_devices.bit_length() - 1
    device_index = lax.axis_index("ctx")
    bit_list = list(range(seg_bits))
    score_scale = DH ** (-0.5)
    q_sparse = sparse_rows(queries)
    k_sparse = sparse_rows(keys)
    v_sparse = sparse_rows(values)
    gathered = spread(
        jnp.stack([k_sparse, v_sparse], axis=1),
        lambda payload, bit_num: partner_2(payload, "ctx", bit_num),
        bit_list,
        device_index,
    )
    seg_keys = gathered[:, 0]
    seg_values = gathered[:, 1]
    full_weight = lax.all_gather(out_weight, "ctx", axis=0, tiled=True)
    scores = (
        jnp.einsum("qhd,khd->hqk", q_sparse, seg_keys, preferred_element_type=jnp.float32)
        * score_scale
    )
    row_top = jnp.max(scores, axis=-1, keepdims=True)
    log_total = row_top + jnp.log(jnp.sum(jnp.exp(scores - row_top), axis=-1, keepdims=True))
    probability = jnp.exp(scores - log_total)
    attn_sparse = jnp.einsum(
        "hqk,khd->qhd",
        probability.astype(jnp.bfloat16),
        seg_values,
        preferred_element_type=jnp.float32,
    ).astype(jnp.bfloat16)
    attention = dense_rows(attn_sparse)
    projected = lax.dot_general(
        attention, full_weight, (((1,), (1,)), ((), ())), preferred_element_type=jnp.float32
    ).astype(jnp.bfloat16)
    weight_grad = lax.psum_scatter(
        lax.dot_general(
            cotangent, attention, (((0,), (0,)), ((), ())), preferred_element_type=jnp.float32
        ),
        "ctx",
        scatter_dimension=0,
        tiled=True,
    )
    d_attention = jnp.dot(cotangent, full_weight, preferred_element_type=jnp.float32).astype(
        jnp.bfloat16
    )
    da_sparse = sparse_rows(d_attention)
    row_delta = jnp.sum(da_sparse.astype(jnp.float32) * attn_sparse.astype(jnp.float32), axis=-1)
    prob_grad = jnp.einsum(
        "qhd,khd->hqk", da_sparse, seg_values, preferred_element_type=jnp.float32
    )
    score_grad = (probability * (prob_grad - row_delta.T[:, :, None])).astype(jnp.bfloat16)
    query_part = (
        jnp.einsum("hqk,khd->qhd", score_grad, seg_keys, preferred_element_type=jnp.float32)
        * score_scale
    ).astype(jnp.bfloat16)
    row_stats = jnp.stack([log_total[:, :, 0].T, row_delta], axis=1)
    seg_stats = spread(
        row_stats,
        lambda payload, bit_num: partner_2(payload, "ctx", bit_num),
        bit_list,
        device_index,
    )
    paired = spread(
        jnp.stack([q_sparse, da_sparse], axis=1),
        lambda payload, bit_num: partner_2(payload, "ctx", bit_num),
        bit_list,
        device_index,
    )
    seg_queries = paired[:, 0]
    seg_cotangent = paired[:, 1]
    key_scores = (
        jnp.einsum("qhd,khd->hqk", seg_queries, k_sparse, preferred_element_type=jnp.float32)
        * score_scale
    )
    key_prob = jnp.exp(key_scores - seg_stats[:, 0].T[:, :, None])
    key_dgrad = jnp.einsum(
        "qhd,khd->hqk", seg_cotangent, v_sparse, preferred_element_type=jnp.float32
    )
    key_dscore = (key_prob * (key_dgrad - seg_stats[:, 1].T[:, :, None])).astype(jnp.bfloat16)
    key_part = (
        jnp.einsum("hqk,qhd->khd", key_dscore, seg_queries, preferred_element_type=jnp.float32)
        * score_scale
    ).astype(jnp.bfloat16)
    value_part = jnp.einsum(
        "hqk,qhd->khd",
        key_prob.astype(jnp.bfloat16),
        seg_cotangent,
        preferred_element_type=jnp.float32,
    ).astype(jnp.bfloat16)
    return (
        projected,
        weight_grad,
        dense_rows(query_part),
        dense_rows(key_part),
        dense_rows(value_part),
    )


LANES = 128
D = H * DH
F32 = jnp.float32
BF16 = jnp.bfloat16


def fits(mesh):
    return mesh.shape["ctx"] * LANES == D


def mm(a, b, dims):
    return lax.dot_general(a, b, (dims, ((), ())), preferred_element_type=F32)


NN = ((1,), (0,))
NT = ((1,), (1,))
TN = ((0,), (0,))


def fused_kernel(
    n, rows,
    q_hbm, k_hbm, v_hbm, c_hbm, w_hbm,
    pr_recv, dg_recv, wg_any,
    q_v, k_v, v_v, c_v, w_v,
    qkv_send, qkv_recv, cot_send, cot_recv, attn_recv, da_send, da_recv, da_mate, da_from_mate,
    pr_send, dg_send, attn2, wg_out,
    send_sem, recv_sem, in_sem, out_sem,
):
    per = rows // R
    group = 2 * per
    seg_devices = n // 2
    total = n * per
    me = lax.axis_index("ctx")
    peers = [lax.rem(me + d, n) for d in range(n)]
    sources = [lax.rem(me + n - d, n) for d in range(n)]
    mate = me + 1 - 2 * lax.rem(me, 2)
    far_first = sorted(range(1, n), key=lambda d: abs(d - n // 2))

    barrier = pltpu.get_barrier_semaphore()
    for d in range(1, n):
        pl.semaphore_signal(
            barrier, inc=1, device_id={"ctx": peers[d]}, device_id_type=pl.DeviceIdType.MESH
        )
    loads = [
        pltpu.make_async_copy(src, dst, in_sem.at[i])
        for i, (src, dst) in enumerate(
            [(q_hbm, q_v), (k_hbm, k_v), (v_hbm, v_v), (c_hbm, c_v), (w_hbm, w_v)]
        )
    ]
    for load in loads:
        load.start()

    def remote(kind, d, src, dst, to=None):
        return pltpu.make_async_remote_copy(
            src_ref=src,
            dst_ref=dst,
            send_sem=send_sem.at[kind, d],
            recv_sem=recv_sem.at[kind, d],
            device_id={"ctx": peers[d] if to is None else to},
            device_id_type=pl.DeviceIdType.MESH,
        )

    row_id = lax.broadcasted_iota(jnp.int32, (rows, rows), 0)
    col_id = lax.broadcasted_iota(jnp.int32, (rows, rows), 1)
    order = (col_id == R * (row_id % per) + row_id // per).astype(F32).astype(BF16)
    left_row = lax.broadcasted_iota(jnp.int32, (1, LANES), 1) < DH

    for load in loads[:3]:
        load.wait()
    for c in range(n):
        cols = pl.ds(c * LANES, LANES)
        picker = order[c * group : (c + 1) * group, :]
        parts = []
        for ref in (q_v, k_v, v_v):
            picked = mm(picker, ref[:, cols], NN)
            parts.append(jnp.where(left_row, picked[:per], picked[per:]))
        parts.append(jnp.zeros_like(parts[0]))
        qkv_send[c] = jnp.concatenate(parts, axis=0).astype(BF16)
    qkv_recv[me] = qkv_send[me]
    pl.semaphore_wait(barrier, n - 1)
    qkv_copies = [remote(0, d, qkv_send.at[peers[d]], qkv_recv.at[me]) for d in far_first]
    for copy in qkv_copies:
        copy.start()

    def tile(c):
        return pl.ds(pl.multiple_of(c * LANES, LANES), LANES)

    loads[3].wait()
    cot_copies = []
    for d in far_first:
        cot_send[d] = mm(order, c_v[:, tile(peers[d])], NN).astype(BF16)
        copy = remote(1, d, cot_send.at[d], cot_recv.at[me])
        copy.start()
        cot_copies.append(copy)
    cot_recv[me] = mm(order, c_v[:, tile(me)], NN).astype(BF16)
    loads[4].wait()

    for copy in qkv_copies:
        copy.wait_recv()
    got = qkv_recv[...].astype(F32)

    def taken(j):
        return got[:, j * per : (j + 1) * per, :].reshape(total, LANES)

    def split(x):
        zero = jnp.zeros_like(x)
        return jnp.concatenate(
            [jnp.where(left_row, x, zero), jnp.where(left_row, zero, x)], axis=0
        )

    def joined(x):
        return jnp.where(left_row, x[:total], x[total:])

    scale = DH ** (-0.5)
    q_two = split(taken(0)).astype(BF16)
    k_all = taken(1).astype(BF16)
    v_all = taken(2).astype(BF16)
    seg_rows = seg_devices * per
    q_seg = (lax.broadcasted_iota(jnp.int32, (2 * total, total), 0) % total) // seg_rows
    k_seg = lax.broadcasted_iota(jnp.int32, (2 * total, total), 1) // seg_rows
    same = q_seg == k_seg
    scores = jnp.where(same, mm(q_two, k_all, NT) * scale, -jnp.inf)
    raised = jnp.exp(scores - jnp.max(scores, axis=-1, keepdims=True))
    prob = raised / jnp.sum(raised, axis=-1, keepdims=True)
    prob_16 = prob.astype(BF16)
    attn = joined(mm(prob_16, v_all, NN)).astype(BF16)
    attn_recv[me] = attn
    across = [remote(2, d, attn_recv.at[me], attn_recv.at[me]) for d in range(2, n, 2)]
    to_mate = remote(2, 1, attn_recv.at[me], attn_recv.at[me], mate)
    for copy in across + [to_mate]:
        copy.start()
    for copy in cot_copies:
        copy.wait_recv()

    def cot_group(c):
        picked = cot_recv[:, pl.ds(pl.multiple_of(c * group, group), group), :]
        return picked.reshape(n * group, LANES)

    def da_share(c):
        both = mm(cot_group(c), w_v[:, tile(c)], NN).reshape(n, 2, per, LANES)
        return jnp.where(left_row, both[:, 0], both[:, 1]).reshape(total, LANES)

    chips = n // 2
    for t in range(chips):
        da_mate[t] = da_share(lax.rem(mate + 2 * t, n)).astype(BF16)
    mate_copy = remote(3, 1, da_mate, da_from_mate, mate)
    mate_copy.start()
    shares = [da_share(peers[2 * t]) for t in range(chips)]
    passed = []
    for i, d in enumerate(range(2, n, 2)):
        across[i].wait_recv()
        c = sources[d]
        copy = remote(2, d + 1, attn_recv.at[c], attn_recv.at[c], mate)
        copy.start()
        passed.append(copy)
    attn_copies = across + [to_mate] + passed

    mate_copy.wait_recv()
    da_copies = []
    for t in range(1, chips):
        da_send[t] = (shares[t] + da_from_mate[t].astype(F32)).astype(BF16)
        copy = remote(3, 2 * t, da_send.at[t], da_recv.at[t])
        copy.start()
        da_copies.append(copy)
    own_da = shares[0] + da_from_mate[0].astype(F32)

    pairs = [sources[d] for d in range(0, n, 2)] + [lax.rem(mate + n - d, n) for d in range(0, n, 2)]
    for d, c in enumerate(pairs):
        if d == chips:
            to_mate.wait_recv()
        elif d > chips:
            passed[d - chips - 1].wait_recv()
        packed = attn_recv[c].astype(F32).reshape(n, per, LANES)
        zero = jnp.zeros_like(packed)
        wide = jnp.stack([jnp.where(left_row, packed, zero), jnp.where(left_row, zero, packed)], axis=1)
        wide = wide.reshape(n * group, LANES).astype(BF16)
        attn2[d] = wide
        out = mm(wide, w_v[:, tile(c)], NT).astype(BF16)
        pr_send[:, pl.ds(pl.multiple_of(c * group, group), group), :] = out.reshape(n, group, LANES)
    keep_pr = pltpu.make_async_copy(pr_send.at[me], pr_recv.at[me], out_sem.at[0])
    keep_pr.start()
    pr_copies = [remote(4, d, pr_send.at[peers[d]], pr_recv.at[me]) for d in far_first]
    for copy in pr_copies:
        copy.start()

    for copy in da_copies:
        copy.wait_recv()
    da = own_da
    for t in range(1, chips):
        da = da + da_recv[t].astype(F32)
    da_two = split(da).astype(BF16)
    attn_two = split(attn.astype(F32))
    delta = jnp.sum(da_two.astype(F32) * attn_two, axis=-1, keepdims=True)
    d_score = (prob * (mm(da_two, v_all, NT) - delta)).astype(BF16)
    dq = joined(mm(d_score, k_all, NN)) * scale
    dk = mm(d_score, q_two, TN) * scale
    dv = mm(prob_16, da_two, TN)
    grads = [g.reshape(n, per, LANES) for g in (dq, dk, dv)]
    grads.append(jnp.zeros_like(grads[0]))
    dg_send[...] = jnp.concatenate(grads, axis=1).astype(BF16)
    keep_dg = pltpu.make_async_copy(dg_send.at[me], dg_recv.at[me], out_sem.at[1])
    keep_dg.start()
    dg_copies = [remote(5, d, dg_send.at[peers[d]], dg_recv.at[me]) for d in range(1, n)]
    for copy in dg_copies:
        copy.start()

    for d, c in enumerate(pairs):
        wg_out[:, tile(c)] = mm(cot_group(c), attn2[d], TN)
    keep_wg = pltpu.make_async_copy(wg_out, wg_any, out_sem.at[2])
    keep_wg.start()

    for copy in pr_copies + dg_copies:
        copy.wait_recv()
    for copy in qkv_copies + cot_copies + attn_copies + [mate_copy] + da_copies + pr_copies + dg_copies:
        copy.wait_send()
    for keep in (keep_pr, keep_dg, keep_wg):
        keep.wait()


def finish_kernel(
    n, rows,
    pr_any, dg_any, wg_any,
    proj_hbm, wg_hbm, dq_hbm, dk_hbm, dv_hbm,
    pr_v, dg_v, wg_v, pr_out, dq_out, dk_out, dv_out, in_sem, out_sem,
):
    per = rows // R
    load_pr = pltpu.make_async_copy(pr_any, pr_v, in_sem.at[0])
    load_dg = pltpu.make_async_copy(dg_any, dg_v, in_sem.at[1])
    load_wg = pltpu.make_async_copy(wg_any, wg_v, in_sem.at[2])
    load_dg.start()
    load_pr.start()
    load_wg.start()
    stores = [
        pltpu.make_async_copy(src, dst, out_sem.at[i])
        for i, (src, dst) in enumerate(
            [(wg_v, wg_hbm), (pr_out, proj_hbm), (dq_out, dq_hbm), (dk_out, dk_hbm), (dv_out, dv_hbm)]
        )
    ]
    load_dg.wait()
    head = lax.broadcasted_iota(jnp.int32, (R, LANES), 0)
    lane_head = lax.broadcasted_iota(jnp.int32, (R, LANES), 1) // DH
    for j, out in enumerate((dq_out, dk_out, dv_out)):
        for c in range(n):
            block = dg_v[c].astype(F32)[j * per : (j + 1) * per]
            here = (lane_head + 2 * c == head)[None]
            spread_out = jnp.where(here, block[:, None, :], 0.0)
            out[:, c * LANES : (c + 1) * LANES] = spread_out.reshape(rows, LANES).astype(BF16)
        stores[2 + j].start()
    row_id = lax.broadcasted_iota(jnp.int32, (rows, rows), 0)
    col_id = lax.broadcasted_iota(jnp.int32, (rows, rows), 1)
    order = (row_id == R * (col_id % per) + col_id // per).astype(F32).astype(BF16)
    load_wg.wait()
    stores[0].start()
    load_pr.wait()
    for c in range(n):
        pr_out[:, c * LANES : (c + 1) * LANES] = mm(order, pr_v[c], NN).astype(BF16)
    stores[1].start()
    for store in stores:
        store.wait()


def fused(queries, keys, values, cotangent, out_weight):
    n = lax.axis_size("ctx")
    rows = queries.shape[0]
    per = rows // R
    total = n * per
    full = (rows, D)
    square = (n, rows, LANES)
    compact = (n, 4 * per, LANES)
    packed = (n, total, LANES)
    half = (n // 2, total, LANES)
    anywhere = pl.BlockSpec(memory_space=pl.ANY)
    in_hbm = pl.BlockSpec(memory_space=pltpu.HBM)
    room = 60 * 1024 * 1024
    pieces = pl.pallas_call(
        functools.partial(fused_kernel, n, rows),
        out_shape=(
            jax.ShapeDtypeStruct(square, BF16),
            jax.ShapeDtypeStruct(compact, BF16),
            jax.ShapeDtypeStruct((D // n, D), F32),
        ),
        in_specs=[in_hbm] * 5,
        out_specs=[anywhere] * 3,
        scratch_shapes=[pltpu.VMEM(full, BF16)] * 4
        + [
            pltpu.VMEM((D // n, D), BF16),
            pltpu.VMEM(compact, BF16),
            pltpu.VMEM(compact, BF16),
            pltpu.VMEM(square, BF16),
            pltpu.VMEM(square, BF16),
            pltpu.VMEM(packed, BF16),
            pltpu.VMEM(half, BF16),
            pltpu.VMEM(half, BF16),
            pltpu.VMEM(half, BF16),
            pltpu.VMEM(half, BF16),
            pltpu.VMEM(square, BF16),
            pltpu.VMEM(compact, BF16),
            pltpu.VMEM((n, n * 2 * per, LANES), BF16),
            pltpu.VMEM((D // n, D), F32),
            pltpu.SemaphoreType.DMA((6, n)),
            pltpu.SemaphoreType.DMA((6, n)),
            pltpu.SemaphoreType.DMA((5,)),
            pltpu.SemaphoreType.DMA((3,)),
        ],
        compiler_params=pltpu.CompilerParams(
            collective_id=0, has_side_effects=True, vmem_limit_bytes=room
        ),
    )(queries, keys, values, cotangent, out_weight)
    return pl.pallas_call(
        functools.partial(finish_kernel, n, rows),
        out_shape=(
            jax.ShapeDtypeStruct(full, BF16),
            jax.ShapeDtypeStruct((D // n, D), F32),
            jax.ShapeDtypeStruct(full, BF16),
            jax.ShapeDtypeStruct(full, BF16),
            jax.ShapeDtypeStruct(full, BF16),
        ),
        in_specs=[anywhere] * 3,
        out_specs=[in_hbm] * 5,
        scratch_shapes=[pltpu.VMEM(square, BF16), pltpu.VMEM(compact, BF16), pltpu.VMEM((D // n, D), F32)]
        + [pltpu.VMEM(full, BF16)] * 4
        + [pltpu.SemaphoreType.DMA((3,)), pltpu.SemaphoreType.DMA((5,))],
        compiler_params=pltpu.CompilerParams(vmem_limit_bytes=room),
    )(*pieces)


def solution(mesh):
    in_specs = (
        P(("dp", "ctx"), None),
        P(("dp", "ctx"), None),
        P(("dp", "ctx"), None),
        P(("dp", "ctx"), None),
        P("ctx", None),
    )
    out_specs = (
        P(("dp", "ctx"), None),
        P(("dp", "ctx"), None),
        P(("dp", "ctx"), None),
        P(("dp", "ctx"), None),
        P(("dp", "ctx"), None),
    )
    body = fused if fits(mesh) else shards
    return jax.shard_map(body, mesh=mesh, in_specs=in_specs, out_specs=out_specs, check_vma=False)
```

```python
import functools

import jax
import jax.numpy as jnp
from jax import lax
from jax.experimental import pallas as pl
from jax.experimental.pallas import tpu as pltpu
from jax.sharding import PartitionSpec as P

H = 16
DH = 64
R = 16


def partner_2(value, axis, apart):
    mask = 2**apart
    pairs = [(source, source ^ mask) for source in range(lax.axis_size(axis))]
    return lax.ppermute(value, axis, pairs)


def select_mask(dtype):
    residue = jnp.arange(R)[:, None]
    head_ids = jnp.arange(H)[None, :]
    return (head_ids % R == residue).astype(dtype)[:, :, None]


def sparse_rows(full_rows):
    reshaped = full_rows.reshape(full_rows.shape[0] // R, R, H, DH)
    return jnp.sum(reshaped * select_mask(full_rows.dtype), axis=1)


def dense_rows(sparse):
    placed = sparse[:, None, :, :] * select_mask(sparse.dtype)
    return placed.reshape(sparse.shape[0] * R, H * DH)


def spread(payload, swapper, bit_list, device_index):
    visited = []
    gathered = payload
    for bit_num in bit_list:
        partner = swapper(gathered, bit_num)
        upper_half = device_index // (1 << bit_num) % 2 == 1
        gathered = jnp.where(
            upper_half, jnp.stack([partner, gathered]), jnp.stack([gathered, partner])
        )
        visited.insert(0, bit_num)
    axis_order = [visited.index(bit_num) for bit_num in sorted(visited, reverse=True)]
    trailing = list(range(len(visited), gathered.ndim))
    gathered = jnp.transpose(gathered, axis_order + trailing)
    return gathered.reshape((-1,) + payload.shape[1:])


def shards(queries, keys, values, cotangent, out_weight):
    ctx_size = lax.axis_size("ctx")
    seg_devices = min(64, ctx_size // 2)
    seg_bits = seg_devices.bit_length() - 1
    device_index = lax.axis_index("ctx")
    bit_list = list(range(seg_bits))
    score_scale = DH ** (-0.5)
    q_sparse = sparse_rows(queries)
    k_sparse = sparse_rows(keys)
    v_sparse = sparse_rows(values)
    gathered = spread(
        jnp.stack([k_sparse, v_sparse], axis=1),
        lambda payload, bit_num: partner_2(payload, "ctx", bit_num),
        bit_list,
        device_index,
    )
    seg_keys = gathered[:, 0]
    seg_values = gathered[:, 1]
    full_weight = lax.all_gather(out_weight, "ctx", axis=0, tiled=True)
    scores = (
        jnp.einsum("qhd,khd->hqk", q_sparse, seg_keys, preferred_element_type=jnp.float32)
        * score_scale
    )
    row_top = jnp.max(scores, axis=-1, keepdims=True)
    log_total = row_top + jnp.log(jnp.sum(jnp.exp(scores - row_top), axis=-1, keepdims=True))
    probability = jnp.exp(scores - log_total)
    attn_sparse = jnp.einsum(
        "hqk,khd->qhd",
        probability.astype(jnp.bfloat16),
        seg_values,
        preferred_element_type=jnp.float32,
    ).astype(jnp.bfloat16)
    attention = dense_rows(attn_sparse)
    projected = lax.dot_general(
        attention, full_weight, (((1,), (1,)), ((), ())), preferred_element_type=jnp.float32
    ).astype(jnp.bfloat16)
    weight_grad = lax.psum_scatter(
        lax.dot_general(
            cotangent, attention, (((0,), (0,)), ((), ())), preferred_element_type=jnp.float32
        ),
        "ctx",
        scatter_dimension=0,
        tiled=True,
    )
    d_attention = jnp.dot(cotangent, full_weight, preferred_element_type=jnp.float32).astype(
        jnp.bfloat16
    )
    da_sparse = sparse_rows(d_attention)
    row_delta = jnp.sum(da_sparse.astype(jnp.float32) * attn_sparse.astype(jnp.float32), axis=-1)
    prob_grad = jnp.einsum(
        "qhd,khd->hqk", da_sparse, seg_values, preferred_element_type=jnp.float32
    )
    score_grad = (probability * (prob_grad - row_delta.T[:, :, None])).astype(jnp.bfloat16)
    query_part = (
        jnp.einsum("hqk,khd->qhd", score_grad, seg_keys, preferred_element_type=jnp.float32)
        * score_scale
    ).astype(jnp.bfloat16)
    row_stats = jnp.stack([log_total[:, :, 0].T, row_delta], axis=1)
    seg_stats = spread(
        row_stats,
        lambda payload, bit_num: partner_2(payload, "ctx", bit_num),
        bit_list,
        device_index,
    )
    paired = spread(
        jnp.stack([q_sparse, da_sparse], axis=1),
        lambda payload, bit_num: partner_2(payload, "ctx", bit_num),
        bit_list,
        device_index,
    )
    seg_queries = paired[:, 0]
    seg_cotangent = paired[:, 1]
    key_scores = (
        jnp.einsum("qhd,khd->hqk", seg_queries, k_sparse, preferred_element_type=jnp.float32)
        * score_scale
    )
    key_prob = jnp.exp(key_scores - seg_stats[:, 0].T[:, :, None])
    key_dgrad = jnp.einsum(
        "qhd,khd->hqk", seg_cotangent, v_sparse, preferred_element_type=jnp.float32
    )
    key_dscore = (key_prob * (key_dgrad - seg_stats[:, 1].T[:, :, None])).astype(jnp.bfloat16)
    key_part = (
        jnp.einsum("hqk,qhd->khd", key_dscore, seg_queries, preferred_element_type=jnp.float32)
        * score_scale
    ).astype(jnp.bfloat16)
    value_part = jnp.einsum(
        "hqk,qhd->khd",
        key_prob.astype(jnp.bfloat16),
        seg_cotangent,
        preferred_element_type=jnp.float32,
    ).astype(jnp.bfloat16)
    return (
        projected,
        weight_grad,
        dense_rows(query_part),
        dense_rows(key_part),
        dense_rows(value_part),
    )


LANES = 128
D = H * DH
F32 = jnp.float32
BF16 = jnp.bfloat16


def fits(mesh):
    return mesh.shape["ctx"] * LANES == D


def mm(a, b, dims):
    return lax.dot_general(a, b, (dims, ((), ())), preferred_element_type=F32)


NN = ((1,), (0,))
NT = ((1,), (1,))
TN = ((0,), (0,))


def fused_kernel(
    n, rows,
    q_hbm, k_hbm, v_hbm, c_hbm, w_hbm,
    pr_recv, dg_recv, wg_any,
    q_v, k_v, v_v, c_v, w_v,
    qkv_send, qkv_recv, cot_send, cot_recv, attn_recv, da_send, da_recv, da_mate, da_from_mate,
    pr_send, pr_land, dg_send, attn2, wg_out,
    send_sem, recv_sem, in_sem, out_sem,
):
    per = rows // R
    group = 2 * per
    seg_devices = n // 2
    total = n * per
    me = lax.axis_index("ctx")
    peers = [lax.rem(me + d, n) for d in range(n)]
    sources = [lax.rem(me + n - d, n) for d in range(n)]
    mate = me + 1 - 2 * lax.rem(me, 2)
    far_first = sorted(range(1, n), key=lambda d: abs(d - n // 2))

    barrier = pltpu.get_barrier_semaphore()
    for d in range(1, n):
        pl.semaphore_signal(
            barrier, inc=1, device_id={"ctx": peers[d]}, device_id_type=pl.DeviceIdType.MESH
        )
    loads = [
        pltpu.make_async_copy(src, dst, in_sem.at[i])
        for i, (src, dst) in enumerate(
            [(q_hbm, q_v), (k_hbm, k_v), (v_hbm, v_v), (c_hbm, c_v), (w_hbm, w_v)]
        )
    ]
    for load in loads:
        load.start()

    def remote(kind, d, src, dst, to=None):
        return pltpu.make_async_remote_copy(
            src_ref=src,
            dst_ref=dst,
            send_sem=send_sem.at[kind, d],
            recv_sem=recv_sem.at[kind, d],
            device_id={"ctx": peers[d] if to is None else to},
            device_id_type=pl.DeviceIdType.MESH,
        )

    row_id = lax.broadcasted_iota(jnp.int32, (rows, rows), 0)
    col_id = lax.broadcasted_iota(jnp.int32, (rows, rows), 1)
    order = (col_id == R * (row_id % per) + row_id // per).astype(F32).astype(BF16)
    left_row = lax.broadcasted_iota(jnp.int32, (1, LANES), 1) < DH

    for load in loads[:3]:
        load.wait()
    for c in range(n):
        cols = pl.ds(c * LANES, LANES)
        picker = order[c * group : (c + 1) * group, :]
        parts = []
        for ref in (q_v, k_v, v_v):
            picked = mm(picker, ref[:, cols], NN)
            parts.append(jnp.where(left_row, picked[:per], picked[per:]))
        parts.append(jnp.zeros_like(parts[0]))
        qkv_send[c] = jnp.concatenate(parts, axis=0).astype(BF16)
    qkv_recv[me] = qkv_send[me]
    pl.semaphore_wait(barrier, n - 1)
    qkv_copies = [remote(0, d, qkv_send.at[peers[d]], qkv_recv.at[me]) for d in far_first]
    for copy in qkv_copies:
        copy.start()

    def tile(c):
        return pl.ds(pl.multiple_of(c * LANES, LANES), LANES)

    loads[3].wait()
    cot_copies = []
    for d in far_first:
        cot_send[d] = mm(order, c_v[:, tile(peers[d])], NN).astype(BF16)
        copy = remote(1, d, cot_send.at[d], cot_recv.at[me])
        copy.start()
        cot_copies.append(copy)
    cot_recv[me] = mm(order, c_v[:, tile(me)], NN).astype(BF16)
    loads[4].wait()

    for copy in qkv_copies:
        copy.wait_recv()
    got = qkv_recv[...].astype(F32)

    def taken(j):
        return got[:, j * per : (j + 1) * per, :].reshape(total, LANES)

    def split(x):
        zero = jnp.zeros_like(x)
        return jnp.concatenate(
            [jnp.where(left_row, x, zero), jnp.where(left_row, zero, x)], axis=0
        )

    def joined(x):
        return jnp.where(left_row, x[:total], x[total:])

    scale = DH ** (-0.5)
    q_two = split(taken(0)).astype(BF16)
    k_all = taken(1).astype(BF16)
    v_all = taken(2).astype(BF16)
    seg_rows = seg_devices * per
    q_seg = (lax.broadcasted_iota(jnp.int32, (2 * total, total), 0) % total) // seg_rows
    k_seg = lax.broadcasted_iota(jnp.int32, (2 * total, total), 1) // seg_rows
    same = q_seg == k_seg
    scores = jnp.where(same, mm(q_two, k_all, NT) * scale, -jnp.inf)
    raised = jnp.exp(scores - jnp.max(scores, axis=-1, keepdims=True))
    prob = raised / jnp.sum(raised, axis=-1, keepdims=True)
    prob_16 = prob.astype(BF16)
    attn = joined(mm(prob_16, v_all, NN)).astype(BF16)
    attn_recv[me] = attn
    across = [remote(2, d, attn_recv.at[me], attn_recv.at[me]) for d in range(2, n, 2)]
    to_mate = remote(2, 1, attn_recv.at[me], attn_recv.at[me], mate)
    for copy in across + [to_mate]:
        copy.start()
    for copy in cot_copies:
        copy.wait_recv()

    def cot_group(c):
        picked = cot_recv[:, pl.ds(pl.multiple_of(c * group, group), group), :]
        return picked.reshape(n * group, LANES)

    def da_share(c):
        both = mm(cot_group(c), w_v[:, tile(c)], NN).reshape(n, 2, per, LANES)
        return jnp.where(left_row, both[:, 0], both[:, 1]).reshape(total, LANES)

    chips = n // 2
    for t in range(chips):
        da_mate[t] = da_share(lax.rem(mate + 2 * t, n)).astype(BF16)
    mate_copy = remote(3, 1, da_mate, da_from_mate, mate)
    mate_copy.start()
    shares = [da_share(peers[2 * t]) for t in range(chips)]
    passed = []
    for i, d in enumerate(range(2, n, 2)):
        across[i].wait_recv()
        c = sources[d]
        copy = remote(2, d + 1, attn_recv.at[c], attn_recv.at[c], mate)
        copy.start()
        passed.append(copy)
    attn_copies = across + [to_mate] + passed

    mate_copy.wait_recv()
    da_copies = []
    for t in range(1, chips):
        da_send[t] = (shares[t] + da_from_mate[t].astype(F32)).astype(BF16)
        copy = remote(3, 2 * t, da_send.at[t], da_recv.at[t])
        copy.start()
        da_copies.append(copy)
    own_da = shares[0] + da_from_mate[0].astype(F32)

    pairs = [sources[d] for d in range(0, n, 2)] + [lax.rem(mate + n - d, n) for d in range(0, n, 2)]
    for d, c in enumerate(pairs):
        if d == chips:
            to_mate.wait_recv()
        elif d > chips:
            passed[d - chips - 1].wait_recv()
        packed = attn_recv[c].astype(F32).reshape(n, per, LANES)
        zero = jnp.zeros_like(packed)
        wide = jnp.stack([jnp.where(left_row, packed, zero), jnp.where(left_row, zero, packed)], axis=1)
        wide = wide.reshape(n * group, LANES).astype(BF16)
        attn2[d] = wide
        out = mm(wide, w_v[:, tile(c)], NT).astype(BF16)
        pr_send[:, pl.ds(pl.multiple_of(c * group, group), group), :] = out.reshape(n, group, LANES)
    pr_land[me] = pr_send[me]
    pr_copies = [remote(4, d, pr_send.at[peers[d]], pr_land.at[me]) for d in far_first]
    for copy in pr_copies:
        copy.start()

    for copy in da_copies:
        copy.wait_recv()
    da = own_da
    for t in range(1, chips):
        da = da + da_recv[t].astype(F32)
    da_two = split(da).astype(BF16)
    attn_two = split(attn.astype(F32))
    delta = jnp.sum(da_two.astype(F32) * attn_two, axis=-1, keepdims=True)
    d_score = (prob * (mm(da_two, v_all, NT) - delta)).astype(BF16)
    dq = joined(mm(d_score, k_all, NN)) * scale
    dk = mm(d_score, q_two, TN) * scale
    dv = mm(prob_16, da_two, TN)
    grads = [g.reshape(n, per, LANES) for g in (dq, dk, dv)]
    grads.append(jnp.zeros_like(grads[0]))
    dg_send[...] = jnp.concatenate(grads, axis=1).astype(BF16)
    keep_dg = pltpu.make_async_copy(dg_send.at[me], dg_recv.at[me], out_sem.at[1])
    keep_dg.start()
    dg_copies = [remote(5, d, dg_send.at[peers[d]], dg_recv.at[me]) for d in range(1, n)]
    for copy in dg_copies:
        copy.start()

    for d, c in enumerate(pairs):
        wg_out[:, tile(c)] = mm(cot_group(c), attn2[d], TN)
    keep_wg = pltpu.make_async_copy(wg_out, wg_any, out_sem.at[2])
    keep_wg.start()

    for copy in pr_copies:
        copy.wait_recv()
    keep_pr = pltpu.make_async_copy(pr_land, pr_recv, out_sem.at[0])
    keep_pr.start()
    for copy in dg_copies:
        copy.wait_recv()
    for copy in qkv_copies + cot_copies + attn_copies + [mate_copy] + da_copies + pr_copies + dg_copies:
        copy.wait_send()
    for keep in (keep_pr, keep_dg, keep_wg):
        keep.wait()


def finish_kernel(
    n, rows,
    pr_any, dg_any, wg_any,
    proj_hbm, wg_hbm, dq_hbm, dk_hbm, dv_hbm,
    pr_v, dg_v, wg_v, pr_out, dq_out, dk_out, dv_out, in_sem, out_sem,
):
    per = rows // R
    load_pr = pltpu.make_async_copy(pr_any, pr_v, in_sem.at[0])
    load_dg = pltpu.make_async_copy(dg_any, dg_v, in_sem.at[1])
    load_wg = pltpu.make_async_copy(wg_any, wg_v, in_sem.at[2])
    load_dg.start()
    load_pr.start()
    load_wg.start()
    stores = [
        pltpu.make_async_copy(src, dst, out_sem.at[i])
        for i, (src, dst) in enumerate(
            [(wg_v, wg_hbm), (pr_out, proj_hbm), (dq_out, dq_hbm), (dk_out, dk_hbm), (dv_out, dv_hbm)]
        )
    ]
    load_dg.wait()
    head = lax.broadcasted_iota(jnp.int32, (R, LANES), 0)
    lane_head = lax.broadcasted_iota(jnp.int32, (R, LANES), 1) // DH
    for j, out in enumerate((dq_out, dk_out, dv_out)):
        for c in range(n):
            block = dg_v[c].astype(F32)[j * per : (j + 1) * per]
            here = (lane_head + 2 * c == head)[None]
            spread_out = jnp.where(here, block[:, None, :], 0.0)
            out[:, c * LANES : (c + 1) * LANES] = spread_out.reshape(rows, LANES).astype(BF16)
        stores[2 + j].start()
    row_id = lax.broadcasted_iota(jnp.int32, (rows, rows), 0)
    col_id = lax.broadcasted_iota(jnp.int32, (rows, rows), 1)
    order = (row_id == R * (col_id % per) + col_id // per).astype(F32).astype(BF16)
    load_wg.wait()
    stores[0].start()
    load_pr.wait()
    for c in range(n):
        pr_out[:, c * LANES : (c + 1) * LANES] = mm(order, pr_v[c], NN).astype(BF16)
    stores[1].start()
    for store in stores:
        store.wait()


def fused(queries, keys, values, cotangent, out_weight):
    n = lax.axis_size("ctx")
    rows = queries.shape[0]
    per = rows // R
    total = n * per
    full = (rows, D)
    square = (n, rows, LANES)
    compact = (n, 4 * per, LANES)
    packed = (n, total, LANES)
    half = (n // 2, total, LANES)
    anywhere = pl.BlockSpec(memory_space=pl.ANY)
    in_hbm = pl.BlockSpec(memory_space=pltpu.HBM)
    room = 60 * 1024 * 1024
    pieces = pl.pallas_call(
        functools.partial(fused_kernel, n, rows),
        out_shape=(
            jax.ShapeDtypeStruct(square, BF16),
            jax.ShapeDtypeStruct(compact, BF16),
            jax.ShapeDtypeStruct((D // n, D), F32),
        ),
        in_specs=[in_hbm] * 5,
        out_specs=[anywhere] * 3,
        scratch_shapes=[pltpu.VMEM(full, BF16)] * 4
        + [
            pltpu.VMEM((D // n, D), BF16),
            pltpu.VMEM(compact, BF16),
            pltpu.VMEM(compact, BF16),
            pltpu.VMEM(square, BF16),
            pltpu.VMEM(square, BF16),
            pltpu.VMEM(packed, BF16),
            pltpu.VMEM(half, BF16),
            pltpu.VMEM(half, BF16),
            pltpu.VMEM(half, BF16),
            pltpu.VMEM(half, BF16),
            pltpu.VMEM(square, BF16),
            pltpu.VMEM(square, BF16),
            pltpu.VMEM(compact, BF16),
            pltpu.VMEM((n, n * 2 * per, LANES), BF16),
            pltpu.VMEM((D // n, D), F32),
            pltpu.SemaphoreType.DMA((6, n)),
            pltpu.SemaphoreType.DMA((6, n)),
            pltpu.SemaphoreType.DMA((5,)),
            pltpu.SemaphoreType.DMA((3,)),
        ],
        compiler_params=pltpu.CompilerParams(
            collective_id=0, has_side_effects=True, vmem_limit_bytes=room
        ),
    )(queries, keys, values, cotangent, out_weight)
    return pl.pallas_call(
        functools.partial(finish_kernel, n, rows),
        out_shape=(
            jax.ShapeDtypeStruct(full, BF16),
            jax.ShapeDtypeStruct((D // n, D), F32),
            jax.ShapeDtypeStruct(full, BF16),
            jax.ShapeDtypeStruct(full, BF16),
            jax.ShapeDtypeStruct(full, BF16),
        ),
        in_specs=[anywhere] * 3,
        out_specs=[in_hbm] * 5,
        scratch_shapes=[pltpu.VMEM(square, BF16), pltpu.VMEM(compact, BF16), pltpu.VMEM((D // n, D), F32)]
        + [pltpu.VMEM(full, BF16)] * 4
        + [pltpu.SemaphoreType.DMA((3,)), pltpu.SemaphoreType.DMA((5,))],
        compiler_params=pltpu.CompilerParams(vmem_limit_bytes=room),
    )(*pieces)


def solution(mesh):
    in_specs = (
        P(("dp", "ctx"), None),
        P(("dp", "ctx"), None),
        P(("dp", "ctx"), None),
        P(("dp", "ctx"), None),
        P("ctx", None),
    )
    out_specs = (
        P(("dp", "ctx"), None),
        P(("dp", "ctx"), None),
        P(("dp", "ctx"), None),
        P(("dp", "ctx"), None),
        P(("dp", "ctx"), None),
    )
    body = fused if fits(mesh) else shards
    return jax.shard_map(body, mesh=mesh, in_specs=in_specs, out_specs=out_specs, check_vma=False)
```
